128 devices in a mesh: row: 32 (over z, y, x_hi), col: 4 (over x_lo, core).
Axes of the slice: x: 4 (x_hi: 2, x_lo: 2; x = x_hi * 2 + x_lo), y: 4, z: 4, core: 2. Of those that a mesh axis runs over, the one named last changes fastest.
Arguments:
- rhs_child: float32 [256, 131072], P(None, ('row', 'col')), may hold values from -8 to 8
- rhs_parent: float32 [256, 131072], P('col', 'row'), may hold values from -8 to 8
- dinv_child: bfloat16 [131072, 4096], P('row', 'col'), may hold values from -0.09375 to 0.09375
- dinv_parent: bfloat16 [131072, 4096], P('row', 'col'), may hold values from -0.09375 to 0.09375
- ubase_child: bfloat16 [64, 131072], P(None, ('row', 'col')), may hold values from -0.09375 to 0.09375
- vbase_child: bfloat16 [64, 131072], P(None, ('row', 'col')), may hold values from -0.09375 to 0.09375
- ubase_parent: bfloat16 [64, 131072], P(None, ('row', 'col')), may hold values from -0.09375 to 0.09375
- vbase_parent: bfloat16 [64, 131072], P(None, ('row', 'col')), may hold values from -0.09375 to 0.09375
- trans_child: float32 [32, 64, 64], P('row'), may hold values from -1 to 2
- trans_parent: float32 [32, 64, 64], P('row'), may hold values from -1 to 2
- w_first: bfloat16 [64, 131072], P(None, ('row', 'col')), may hold values from -0.5 to 0.5
- w_second: bfloat16 [32, 262144], P(None, 'row'), may hold values from -1 to 1
- block_ranks: int32 [1024], P(('row', 'col')), may hold values from 16 to 64
- extend_map: int32 [2048], replicated, may hold values from 0 to 1023, as said below
Outputs:
- x_child: float32 [256, 131072], P(None, ('row', 'col'))
- x_parent: float32 [256, 131072], P(None, ('row', 'col'))
The draws below stay inside these ranges and needn't reach their ends.
Inputs may be any that keep to these rules, and one draw needn't show every extreme that they name: `extend_map`: entries i * 64 to i * 64 + 63 belong to row index i. The entries of the first half of the row indices name every parent block exactly once, and so do those of the second half. Parent block p is held by row index p // 32. From one row index, 0, half of 4, or 4 entries name blocks held by one row index, and every row index sends 4 to some row index.
All inputs are finite; a program needn't handle non-finite values.
Results may differ from the reference program's by a relative error of at most 0.028.
Values may be sent and summed in bfloat16 or wider, within the bound.
A program may use at most 128 MiB of HBM per device.

```python
import math
import jax
import jax.numpy as jnp
from jax import lax

NRHS = 256
NB = 4096
BLK = 128
R = 64
NG = 32
RPAD = 64
UB = 64
NP = 131072
N_ROW = 32


def transitions(key, series_extent, lasting_share):
    stochastic_split_keys = jax.random.split(key, 7)
    lasting_indicators = jax.random.uniform(stochastic_split_keys[0], (R,)) < lasting_share
    slow_log = math.log(0.1) * jax.random.uniform(stochastic_split_keys[1], (R,), minval=0.15, maxval=0.6) / series_extent
    fast_log = jnp.log(jax.random.uniform(stochastic_split_keys[2], (R,), minval=0.15, maxval=0.5))
    base_log = jnp.where(lasting_indicators, slow_log, fast_log)
    spread = jnp.exp(jax.random.uniform(stochastic_split_keys[3], (N_ROW, R), minval=math.log(0.6), maxval=math.log(1.5)))
    arrival_intensities = jnp.exp(base_log[None, :] * spread)
    clustered_arrivals = jax.random.uniform(stochastic_split_keys[4], (N_ROW, 1)) < 2.0 / series_extent
    discarded_values = jax.random.uniform(stochastic_split_keys[5], (N_ROW, R), minval=0.55, maxval=0.85)
    arrival_intensities = jnp.where(clustered_arrivals & lasting_indicators[None, :], arrival_intensities * discarded_values, arrival_intensities)
    noise = jnp.clip(jax.random.normal(stochastic_split_keys[6], (N_ROW, R, R)), -4.0, 4.0) * (0.15 / math.sqrt(R))
    return arrival_intensities[:, :, None] * jnp.eye(R, dtype=jnp.float32)[None, :, :] + noise


def draw_trans_child(key, part):
    key = jax.random.fold_in(key, 21)
    lasting_share = 0.5
    return transitions(key, N_ROW // 2, lasting_share)


def draw_trans_parent(key, part):
    key = jax.random.fold_in(key, 22)
    lasting_share = 0.5
    return transitions(key, N_ROW, lasting_share)


def child_blocks(key):
    sources = N_ROW // 2
    target_slots = N_ROW
    per_target = NB // BLK
    per_source = 2 * per_target
    average = per_source // target_slots
    stochastic_split_keys = jax.random.split(key, 4)
    source_class = jax.random.permutation(stochastic_split_keys[0], jnp.arange(sources, dtype=jnp.int32) % 4)
    target_class = jax.random.permutation(stochastic_split_keys[1], jnp.arange(target_slots, dtype=jnp.int32) % 4)
    source_one = 2 * (source_class % 2) - 1
    source_two = 2 * (source_class // 2) - 1
    target_one = 2 * (target_class % 2) - 1
    target_two = 2 * (target_class // 2) - 1
    counts = average + average // 2 * (source_one[:, None] * target_one[None, :] + source_two[:, None] * target_two[None, :])
    ends = jnp.cumsum(counts, axis=1)
    starts = ends - counts
    places = jnp.arange(per_source, dtype=jnp.int32)
    chosen = jnp.sum(ends[:, None, :] <= places[None, :, None], axis=2, dtype=jnp.int32)
    within = places[None, :] - jnp.take_along_axis(starts, chosen, axis=1)
    offsets = jnp.cumsum(counts, axis=0) - counts
    inside = jnp.take_along_axis(offsets, chosen, axis=1) + within
    target_orders = jax.vmap(lambda subkey: jax.random.permutation(subkey, per_target))(jax.random.split(stochastic_split_keys[2], target_slots)).astype(jnp.int32)
    parent = chosen * per_target + target_orders[chosen, inside]
    source_orders = jax.vmap(lambda subkey: jax.random.permutation(subkey, per_source))(jax.random.split(stochastic_split_keys[3], sources)).astype(jnp.int32)
    inverse = jnp.argsort(source_orders, axis=1)
    return jnp.take_along_axis(parent, inverse, axis=1).reshape(-1)


def draw_extend_map(key, part):
    key = jax.random.fold_in(key, 31)
    first_half = child_blocks(jax.random.fold_in(key, 1))
    second_half = child_blocks(jax.random.fold_in(key, 2))
    return jnp.concatenate([first_half, second_half]).astype(jnp.int32)


def set_ends(values, key, smallest, high):
    longest = values.shape.index(max(values.shape))
    spots = []
    for shift in (0, 1):
        where = [jax.random.randint(jax.random.fold_in(key, axis), (), 0, length) for axis, length in enumerate(values.shape)]
        where[longest] = (where[longest] + shift) % values.shape[longest]
        spots.append(tuple(where))
    return values.at[spots[0]].set(smallest).at[spots[1]].set(high)


def steps_of(stream_key, dims, pieces, smallest, high):
    def one(dim, parts):
        steps = jax.random.uniform(jax.random.fold_in(jax.random.fold_in(stream_key, 6), dim), (parts,), jnp.float32, smallest / len(pieces), high / len(pieces))
        return jnp.repeat(jnp.exp(steps), dims[dim] // parts).reshape((-1,) + (1,) * (len(dims) - dim - 1))

    gain = one(*pieces[0])
    for cut in pieces[1:]:
        gain = gain * one(*cut)
    return gain


def scatter_about(rng, shape, scale, reach, cuts=(), kind=jnp.bfloat16):
    drawn = scale * jax.random.normal(rng, shape, jnp.float32)
    if cuts:
        drawn = drawn * steps_of(rng, shape, cuts, -0.22, 0.18)
    return jnp.clip(drawn, -reach, reach).astype(kind)


def setup_inputs(seed: int = 0) -> dict:
    keys = jax.random.split(jax.random.key(seed), 15)
    rhs_child = scatter_about(keys[0], (NRHS, NP), 1.0, 8.0, ((1, 128),), jnp.float32)
    rhs_parent = scatter_about(keys[1], (NRHS, NP), 1.0, 8.0, ((0, 4), (1, 32)), jnp.float32)
    dinv_child = scatter_about(keys[2], (NP, NB), NB ** -0.5, 0.09375, ((0, 32), (1, 4)))
    dinv_parent = scatter_about(keys[3], (NP, NB), NB ** -0.5, 0.09375, ((0, 32), (1, 4)))
    ubase_child = scatter_about(keys[4], (R, NP), NB ** -0.5, 0.09375, ((1, 128),))
    vbase_child = scatter_about(keys[5], (R, NP), NB ** -0.5, 0.09375, ((1, 128),))
    ubase_parent = scatter_about(keys[6], (R, NP), NB ** -0.5, 0.09375, ((1, 128),))
    vbase_parent = scatter_about(keys[7], (R, NP), NB ** -0.5, 0.09375, ((1, 128),))
    trans_child = draw_trans_child(jax.random.fold_in(keys[14], 71), 0)
    trans_parent = draw_trans_parent(jax.random.fold_in(keys[14], 71), 0)
    w_first = scatter_about(keys[10], (RPAD, NP), BLK ** -0.5, 0.5, ((1, 128),))
    w_second = scatter_about(keys[11], (NG, N_ROW * UB * BLK), NG ** -0.5, 1.0, ((1, 32),))
    block_ranks = set_ends(jax.random.randint(keys[12], (NP // BLK,), RPAD // 4, RPAD + 1), jax.random.fold_in(keys[12], 1), RPAD // 4, RPAD).astype(jnp.int32)
    extend_map = draw_extend_map(jax.random.fold_in(keys[14], 71), 0)
    return dict(rhs_child=rhs_child, rhs_parent=rhs_parent, dinv_child=dinv_child, dinv_parent=dinv_parent, ubase_child=ubase_child, vbase_child=vbase_child, ubase_parent=ubase_parent, vbase_parent=vbase_parent, trans_child=trans_child, trans_parent=trans_parent, w_first=w_first, w_second=w_second, block_ranks=block_ranks, extend_map=extend_map)


PRECISE = lax.Precision.HIGHEST


def blocks_of(matrix, block_rows):
    return matrix.reshape(matrix.shape[0], N_ROW, block_rows).transpose(1, 0, 2)


def lower_solve(inverse_all, left_base, right_base, transfer_all, rhs_all, series_extent):
    inverses = inverse_all.reshape(N_ROW, NB, NB)

    def advance(states, inputs):
        inverse, ublock, vblock, transfer, rhs_block, position = inputs
        retain = jnp.where(position % series_extent == 0, 0.0, 1.0).astype(jnp.float32)
        states = states * retain
        stacked = jnp.concatenate([rhs_block, ublock], axis=0)
        product = jnp.dot(inverse, stacked.T, preferred_element_type=jnp.float32)
        direct = product[:, :NRHS]
        coupled = product[:, NRHS:]
        solved = direct - jnp.dot(coupled, states, precision=PRECISE)
        vfloat = vblock.astype(jnp.float32)
        source = jnp.dot(vfloat, direct, precision=PRECISE)
        kernel = jnp.dot(vfloat, coupled, precision=PRECISE)
        following = jnp.dot(transfer - kernel, states, precision=PRECISE) + source
        return following, solved.T

    initial = jnp.zeros((R, NRHS), jnp.float32)
    positions = jnp.arange(N_ROW, dtype=jnp.int32)
    _, solved = lax.scan(advance, initial, (inverses, blocks_of(left_base, NB), blocks_of(right_base, NB), transfer_all, blocks_of(rhs_all, NB), positions))
    return solved.transpose(1, 0, 2).reshape(NRHS, NP)


def upper_solve(inverse_all, left_base, right_base, transfer_all, rhs_all, series_extent):
    inverses = inverse_all.reshape(N_ROW, NB, NB)

    def advance(states, inputs):
        inverse, ublock, vblock, transfer, rhs_block, position = inputs
        retain = jnp.where(position % series_extent == series_extent - 1, 0.0, 1.0).astype(jnp.float32)
        states = states * retain
        stacked = jnp.concatenate([rhs_block, vblock], axis=0)
        product = jnp.dot(inverse.T, stacked.T, preferred_element_type=jnp.float32)
        direct = product[:, :NRHS]
        coupled = product[:, NRHS:]
        solved = direct - jnp.dot(coupled, states, precision=PRECISE)
        ufloat = ublock.astype(jnp.float32)
        source = jnp.dot(ufloat, direct, precision=PRECISE)
        kernel = jnp.dot(ufloat, coupled, precision=PRECISE)
        following = jnp.dot(transfer.T - kernel, states, precision=PRECISE) + source
        return following, solved.T

    initial = jnp.zeros((R, NRHS), jnp.float32)
    positions = jnp.arange(N_ROW, dtype=jnp.int32)
    _, solved = lax.scan(advance, initial, (inverses, blocks_of(left_base, NB), blocks_of(right_base, NB), transfer_all, blocks_of(rhs_all, NB), positions), reverse=True)
    return solved.transpose(1, 0, 2).reshape(NRHS, NP)


def reference(rhs_child, rhs_parent, dinv_child, dinv_parent, ubase_child, vbase_child, ubase_parent, vbase_parent, trans_child, trans_parent, w_first, w_second, block_ranks, extend_map):
    half_chain = N_ROW // 2
    y_child = lower_solve(dinv_child, ubase_child, vbase_child, trans_child, rhs_child.astype(jnp.bfloat16), half_chain)
    y_round = y_child.astype(jnp.bfloat16)
    rank_index = jnp.arange(RPAD, dtype=jnp.int32)
    allowed = (rank_index[:, None] < block_ranks[None, :]).astype(jnp.float32)
    masked = w_first.astype(jnp.float32).reshape(RPAD, N_ROW, NG, BLK) * allowed.reshape(RPAD, N_ROW, NG)[:, :, :, None]
    y_values = y_round.astype(jnp.float32).reshape(NRHS, N_ROW, NG, BLK)
    factor = jnp.einsum('riga,higa->ighr', masked, y_values).astype(jnp.bfloat16)
    second = w_second.astype(jnp.float32).reshape(NG, N_ROW, UB, BLK)
    update = jnp.einsum('gibw,ighb->ibhw', second, factor.astype(jnp.float32)).astype(jnp.bfloat16)
    parent_count = NP // BLK
    gathered = jnp.zeros((parent_count, NRHS, BLK), jnp.float32).at[extend_map].add(update.reshape(N_ROW * UB, NRHS, BLK).astype(jnp.float32))
    contrib = gathered.transpose(1, 0, 2).reshape(NRHS, NP)
    parent_rhs = (rhs_parent - contrib).astype(jnp.bfloat16)
    y_parent = lower_solve(dinv_parent, ubase_parent, vbase_parent, trans_parent, parent_rhs, N_ROW)
    x_parent = upper_solve(dinv_parent, ubase_parent, vbase_parent, trans_parent, y_parent.astype(jnp.bfloat16), N_ROW)
    x_round = x_parent.astype(jnp.bfloat16)
    parent_blocks = x_round.reshape(NRHS, parent_count, BLK).transpose(1, 0, 2)
    picked = parent_blocks[extend_map].reshape(N_ROW, UB, NRHS, BLK).astype(jnp.float32)
    pulled = jnp.einsum('gibw,ibhw->ighb', second, picked).astype(jnp.bfloat16)
    correction = jnp.einsum('riga,ighr->higa', masked, pulled.astype(jnp.float32)).reshape(NRHS, NP)
    child_z = (y_child - correction).astype(jnp.bfloat16)
    x_child = upper_solve(dinv_child, ubase_child, vbase_child, trans_child, child_z, half_chain)
    return x_child, x_parent
```

```python
from typing import Any, NamedTuple

import jax
import jax.numpy as jnp
from jax import lax
from jax.experimental import pallas as pl
from jax.experimental.pallas import tpu as pltpu
from jax.sharding import PartitionSpec as P

MESH = pl.DeviceIdType.MESH
F32 = jnp.float32
BF16 = jnp.bfloat16
HIGH = lax.Precision.HIGHEST

ROWS = 32
COLS = 4
HALF = 16
H = 256
HS = 64
RANK = 64
NLOC = 1024
GROUPS = 8
BLK = 128
SUBS = 4
SUB = NLOC // SUBS
SLOTS = 4

DMA = pltpu.SemaphoreType.DMA


class Link(NamedTuple):
    src: Any
    dst: Any
    sent: Any
    came: Any


class Hops(NamedTuple):
    buf: Any
    sent: Any
    came: Any


class Sums(NamedTuple):
    a: Link
    b: Link
    acc: Any


class Front(NamedTuple):
    d: Any
    loaded: Any
    ut: Any
    v: Hops
    e: Any
    ehl: Any
    fhl: Any
    bl: Any
    ysum: Sums
    bsum: Sums
    z: Hops
    kern: Link
    maps: Link


class Scan(NamedTuple):
    phi: Any
    phl: Any
    part: Link
    rows: Link
    state: Link


class Route(NamedTuple):
    rows: Link
    cols: Link


class Rest(NamedTuple):
    first: Link
    swap: Link
    sel_s: Any
    sel_st: Any
    sel_r: Any
    sel_rt: Any
    rt: Any
    rpt: Any
    rpb: Any
    y: Any
    yb: Any
    mskt: Any
    fac: Any


def link(src, dst, count, kind=BF16):
    source = None if src is None else pltpu.VMEM(src, kind)
    return Link(source, pltpu.VMEM(dst, kind), DMA((count,)), DMA((count,)))


def sums(subs, rows, lanes):
    two, one = (2 * subs, rows, lanes), (subs, rows, lanes)
    return Sums(link(two, two, 2 * subs), link(one, one, subs), pltpu.VMEM(one, F32))


def front(count):
    return Front(
        d=pltpu.VMEM((COLS, NLOC, NLOC), BF16),
        loaded=DMA((COLS,)),
        ut=pltpu.VMEM((NLOC, RANK), BF16),
        v=Hops(pltpu.VMEM((COLS, RANK, NLOC), BF16), DMA((3, 1)), DMA((3, 1))),
        e=pltpu.VMEM((RANK, NLOC), F32),
        ehl=pltpu.VMEM((2 * RANK, NLOC), BF16),
        fhl=pltpu.VMEM((2 * RANK, NLOC), BF16),
        bl=pltpu.VMEM((NLOC, RANK), BF16),
        ysum=sums(SUBS, SUB, H),
        bsum=sums(1, NLOC // 2, 2 * RANK),
        z=Hops(pltpu.VMEM((COLS, SUBS, H, SUB), BF16), DMA((3, SUBS)), DMA((3, SUBS))),
        kern=link((COLS, RANK, 2 * RANK), (COLS, RANK, 2 * RANK), COLS),
        maps=link(None, (count, RANK, 2 * RANK), count, F32),
    )


def scan(count):
    part = (COLS, RANK // 2, 2 * HS)
    return Scan(
        phi=pltpu.VMEM((count * RANK // 2, 2 * RANK), F32),
        phl=pltpu.VMEM((4 * RANK, count * RANK // 2), BF16),
        part=link(part, part, COLS),
        rows=link(None, (count, RANK // 2, 2 * HS), count),
        state=link(None, part, COLS),
    )


def route(lanes):
    rows, cols = (ROWS, 32, lanes), (COLS, 128, lanes)
    return Route(link(rows, rows, ROWS), link(cols, cols, COLS))


def scratch_tree():
    part = (COLS, RANK // 2, 2 * HS)
    swap = (COLS, HS, NLOC)
    rest = Rest(
        first=link(None, part, COLS),
        swap=link(swap, swap, COLS),
        sel_s=pltpu.VMEM((ROWS * 32, 512), BF16),
        sel_st=pltpu.VMEM((512, ROWS * 32), BF16),
        sel_r=pltpu.VMEM((512, ROWS * 32), BF16),
        sel_rt=pltpu.VMEM((ROWS * 32, 512), BF16),
        rt=pltpu.VMEM((NLOC, H), BF16),
        rpt=pltpu.VMEM((NLOC, H), F32),
        rpb=pltpu.VMEM((NLOC, H), BF16),
        y=pltpu.VMEM((NLOC, H), F32),
        yb=pltpu.VMEM((NLOC, H), BF16),
        mskt=pltpu.VMEM((NLOC, RANK), BF16),
        fac=pltpu.VMEM((512, H), BF16),
    )
    return (
        front(HALF), front(ROWS), scan(ROWS), scan(ROWS), scan(HALF), route(H), route(BLK), route(H), rest,
    )


def dot(a, b):
    return jnp.dot(a, b, preferred_element_type=F32)


def dot_tn(a, b):
    return lax.dot_general(a, b, (((0,), (0,)), ((), ())), preferred_element_type=F32)


def dot_nt(a, b):
    return lax.dot_general(a, b, (((1,), (1,)), ((), ())), preferred_element_type=F32)


def high_low(a):
    high = a.astype(BF16)
    return high, (a - high.astype(F32)).astype(BF16)


def kernel(
    rc, rp, dc_hbm, dp_hbm, uc, vc, up, vp, pc, pp, msk, ws, tgt_row, tgt_col, src_row, src_col,
    xc_out, xp_out, child, parent, ahead, back, child_back, factors, weights, pulled, m,
):
    i = lax.axis_index("row")
    c = lax.axis_index("col")
    peer = c + 1 - 2 * lax.rem(c, 2)
    other = lax.rem(c + 2, COLS)
    diag = lax.rem(peer + 2, COLS)
    loc = lax.rem(i, HALF)
    base = i - loc
    dests = (diag, other, peer, c)
    pending = []

    def remote(src, dst, ss, rs, row, col):
        return pltpu.make_async_remote_copy(
            src_ref=src, dst_ref=dst, send_sem=ss, recv_sem=rs, device_id=(row, col), device_id_type=MESH
        )

    def looped(lo, hi, fn):
        def one(s, carry):
            fn(s)
            return carry

        lax.fori_loop(lo, hi, one, 0)

    def piece_of(ln, here, to):
        return ln.dst.at[here] if ln.src is None else ln.src.at[to]

    def col_copy(ln, d, to, slot):
        return remote(piece_of(ln, c, to), ln.dst.at[slot], ln.sent.at[d], ln.came.at[d], i, to)

    def col_send(ln):
        for d in range(1, COLS):
            col_copy(ln, d, lax.rem(c + d, COLS), c).start()
        pending.append(lambda: [col_copy(ln, d, lax.rem(c + d, COLS), c).wait_send() for d in range(1, COLS)])

    def col_wait(ln):
        for d in range(1, COLS):
            frm = lax.rem(c - d + COLS, COLS)
            col_copy(ln, d, frm, frm).wait_recv()

    def row_place(ln):
        n = ln.dst.shape[0]
        return (n, base, loc) if n == HALF else (n, 0, i)

    def row_copy(ln, d, to, slot):
        _, start, here = row_place(ln)
        return remote(piece_of(ln, here, to), ln.dst.at[slot], ln.sent.at[d], ln.came.at[d], start + to, c)

    def row_send(ln):
        n, _, here = row_place(ln)
        looped(1, n, lambda d: row_copy(ln, d, lax.rem(here + d, n), here).start())
        pending.append(
            lambda: looped(1, n, lambda d: row_copy(ln, d, lax.rem(here + d, n), here).wait_send())
        )

    def row_wait(ln):
        n, _, here = row_place(ln)

        def one(d):
            frm = lax.rem(here - d + n, n)
            row_copy(ln, d, frm, frm).wait_recv()

        looped(1, n, one)

    def hop(hops, step, s, whole=False):
        block = other if step == 2 else c
        to = other if step == 1 else peer
        ref = hops.buf.at[block] if whole else hops.buf.at[block, s]
        return remote(ref, ref, hops.sent.at[step, s], hops.came.at[step, s], i, to)

    def v_start(f, vbase):
        f.v.buf[c] = vbase[...]
        hop(f.v, 1, 0, True).start()
        hop(f.v, 0, 0, True).start()

    def v_forward(f):
        hop(f.v, 1, 0, True).wait_recv()
        hop(f.v, 2, 0, True).start()
        pending.append(lambda: [hop(f.v, step, 0, True).wait_send() for step in range(3)])

    def v_finish(f):
        hop(f.v, 0, 0, True).wait_recv()
        hop(f.v, 2, 0, True).wait_recv()

    def z_start(f, source):
        def one(s):
            piece = source[pl.ds(pl.multiple_of(s * SUB, SUB), SUB), :]
            f.z.buf[c, s] = piece.astype(F32).T.astype(BF16)
            hop(f.z, 1, s).start()
            hop(f.z, 0, s).start()

        looped(0, SUBS, one)
        pending.append(lambda: looped(0, SUBS, lambda s: [hop(f.z, step, s).wait_send() for step in range(3)] and None))

    def z_apply(f, block, out, step):
        def one(s):
            if step is not None:
                hop(f.z, step, s).wait_recv()
                if step == 1:
                    hop(f.z, 2, s).start()
            out[...] += dot(f.z.buf[block, s], f.d[block, pl.ds(pl.multiple_of(s * SUB, SUB), SUB), :])

        if step is None:
            out[...] = jnp.zeros(out.shape, F32)
        looped(0, SUBS, one)

    def within(sm, n):
        return remote(sm.a.src.at[n], sm.a.dst.at[n], sm.a.sent.at[n], sm.a.came.at[n], i, peer)

    def between(sm, n):
        return remote(sm.b.src.at[n], sm.b.dst.at[n], sm.b.sent.at[n], sm.b.came.at[n], i, other)

    def sum_away(sm, piece, ready=lambda n: None):
        subs = sm.acc.shape[0]
        ready(0)

        def first(s):
            sm.a.src[s] = piece(dests[0], s).astype(BF16)
            within(sm, s).start()

        looped(0, subs, first)
        ready(1)

        def second(s):
            own = piece(dests[1], s)
            within(sm, s).wait_recv()
            sm.b.src[s] = (own + sm.a.dst[s].astype(F32)).astype(BF16)
            between(sm, s).start()

        looped(0, subs, second)

    def sum_here(sm, piece):
        subs = sm.acc.shape[0]

        def third(s):
            sm.a.src[subs + s] = piece(dests[2], s).astype(BF16)
            within(sm, subs + s).start()

        looped(0, subs, third)

        def fourth(s):
            sm.acc[s] = piece(dests[3], s)

        looped(0, subs, fourth)

        def each(s):
            within(sm, s).wait_send()
            within(sm, subs + s).wait_send()
            between(sm, s).wait_send()

        pending.append(lambda: looped(0, subs, each))

    def sum_wait(sm, s):
        subs = sm.acc.shape[0]
        within(sm, subs + s).wait_recv()
        between(sm, s).wait_recv()
        return sm.acc[s] + sm.a.dst[subs + s].astype(F32) + sm.b.dst[s].astype(F32)

    def d_piece(f, rhs):
        def piece(dest, s):
            return dot(f.d[dest, pl.ds(pl.multiple_of(s * SUB, SUB), SUB), :], rhs[...])

        return piece

    def b_piece(f):
        def piece(dest, s):
            out = dot(f.d[dest], f.ut[...])
            return jnp.concatenate([out[: NLOC // 2], out[NLOC // 2 :]], axis=1)

        return piece

    def b_finish(f):
        packed = sum_wait(f.bsum, 0)
        out = jnp.concatenate([packed[:, :RANK], packed[:, RANK:]], axis=0)
        f.bl[...] = out.astype(BF16)
        high, low = high_low(out.T)
        f.fhl[:RANK] = high
        f.fhl[RANK:] = low

    def make_e(f):
        def one(b):
            f.e[...] += dot(f.v.buf[b], f.d[b])

        f.e[...] = jnp.zeros((RANK, NLOC), F32)
        looped(0, COLS, one)
        high, low = high_low(f.e[...])
        f.ehl[:RANK] = high
        f.ehl[RANK:] = low

    def project(pair, vec):
        both = dot(pair[...], vec)
        return both[:RANK] + both[RANK:]

    def pack(a):
        return jnp.concatenate([a[: RANK // 2], a[RANK // 2 :]], axis=1)

    def unpack(a):
        return jnp.concatenate([a[:, :HS], a[:, HS:]], axis=0)

    def scan_one(sc, partial):
        for k in range(COLS):
            sc.part.src[k] = pack(partial[:, k * HS : (k + 1) * HS]).astype(BF16)
        col_send(sc.part)

    def scan_two(sc):
        sc.part.dst[c] = sc.part.src[c]
        col_wait(sc.part)
        sc.rows.dst[row_place(sc.rows)[2]] = jnp.sum(sc.part.dst[...].astype(F32), axis=0).astype(BF16)
        row_send(sc.rows)

    def scan_three(sc):
        row_wait(sc.rows)
        both = dot(sc.phl[...], sc.rows.dst[...].reshape(sc.phl.shape[1], 2 * HS))
        both = both[: 2 * RANK] + both[2 * RANK :]
        send_state(sc.state, both[:RANK, :HS] + both[RANK:, HS:])

    def send_state(ln, state):
        ln.dst[c] = pack(state).astype(BF16)
        col_send(ln)

    def wait_state(ln):
        col_wait(ln)
        return jnp.concatenate([unpack(ln.dst[k].astype(F32)) for k in range(COLS)], axis=1).astype(BF16)

    def split_phi(sc):
        high, low = high_low(sc.phi[...].T)
        sc.phl[: 2 * RANK] = high
        sc.phl[2 * RANK :] = low

    def kernel_send(f, kernel_part, source):
        for k in range(COLS):
            left = kernel_part if source is None else source[:, k * HS : (k + 1) * HS]
            f.kern.src[k] = jnp.concatenate([left, kernel_part], axis=1).astype(BF16)
        col_send(f.kern)

    def kernel_sum(f, trans):
        f.kern.dst[c] = f.kern.src[c]
        col_wait(f.kern)
        total = jnp.sum(f.kern.dst[...].astype(F32), axis=0)
        return total[:, :HS], trans[...] - total[:, HS:]

    def maps_send(f, left, right):
        f.maps.dst[row_place(f.maps)[2]] = jnp.concatenate([left, right], axis=1)
        row_send(f.maps)

    def route_rows(rt, values):
        rt.rows.src[...] = values.astype(BF16).reshape(rt.rows.src.shape)
        rt.rows.dst[i] = rt.rows.src[i]
        row_send(rt.rows)

    def route_cols(rt):
        rt.cols.dst[c] = rt.cols.src[c]
        col_send(rt.cols)

    def rows_of(rt):
        row_wait(rt.rows)
        return rt.rows.dst[...].reshape(ROWS * 32, rt.rows.dst.shape[2])

    def onehot(shape, axis, at):
        return (lax.broadcasted_iota(jnp.int32, shape, axis) == at[...]).astype(BF16)

    def load(f, hbm, n):
        return pltpu.make_async_copy(hbm.at[dests[n]], f.d.at[dests[n]], f.loaded.at[n])

    for n in range(COLS):
        load(child, dc_hbm, n).start()
    for n in range(COLS):
        load(parent, dp_hbm, n).start()

    barrier = pltpu.get_barrier_semaphore()

    def greet(row, col):
        pl.semaphore_signal(barrier, inc=1, device_id=(row, col), device_id_type=MESH)

    looped(1, ROWS, lambda d: greet(lax.rem(i + d, ROWS), c))
    for d in range(1, COLS):
        greet(i, lax.rem(c + d, COLS))

    for s in range(SUBS):
        m.rt[s * SUB : (s + 1) * SUB, :] = rc[:, s * SUB : (s + 1) * SUB].T.astype(BF16)
    child.ut[...] = uc[...].astype(F32).T.astype(BF16)
    parent.ut[...] = up[...].astype(F32).T.astype(BF16)
    pl.semaphore_wait(barrier, ROWS + COLS - 2)

    v_start(child, vc)
    y_part = d_piece(child, m.rt)
    sum_away(child.ysum, y_part, lambda n: load(child, dc_hbm, n).wait())
    v_forward(child)
    load(child, dc_hbm, 2).wait()
    load(child, dc_hbm, 3).wait()
    v_finish(child)
    make_e(child)
    kernel_send(child, project(child.ehl, child.ut[...]), project(child.ehl, m.rt[...]))
    sum_here(child.ysum, y_part)
    source, transfer = kernel_sum(child, pc)
    maps_send(child, transfer, source)
    sum_away(child.bsum, b_piece(child))
    sum_here(child.bsum, b_piece(child))

    m.sel_s[...] = onehot((ROWS * 32, 512), 0, tgt_row)
    route_rows(weights, dot(m.sel_s[...], ws[...]))

    row_wait(child.maps)
    eye = (
        lax.broadcasted_iota(jnp.int32, (RANK, RANK), 0) == lax.broadcasted_iota(jnp.int32, (RANK, RANK), 1)
    ).astype(F32)
    left = lax.broadcasted_iota(jnp.int32, (RANK, 2 * RANK), 1) < RANK

    def store_phi(sc, j, value):
        sc.phi[pl.ds(pl.multiple_of(j * (RANK // 2), RANK // 2), RANK // 2), :] = pack(value)

    def child_step(j, both):
        now = child.maps.dst[j]
        product = jnp.dot(now[:, :RANK], both, precision=HIGH)
        added = jnp.concatenate([now[:, RANK:], jnp.zeros((RANK, RANK), F32)], axis=1)
        store_phi(child_back, j, jnp.where(j > loc, both[:, RANK:], 0.0))
        moves = (left & (j < loc)) | (~left & (j > loc))
        return jnp.where(moves, product + added, both)

    both = lax.fori_loop(
        0, HALF, child_step, jnp.concatenate([jnp.zeros((RANK, RANK), F32), eye], axis=1)
    )
    send_state(m.first, both[:, :RANK])
    b_finish(child)
    h_child = wait_state(m.first)

    def child_y(s):
        rows = pl.ds(pl.multiple_of(s * SUB, SUB), SUB)
        value = sum_wait(child.ysum, s) - dot(child.bl[rows, :], h_child)
        m.y[rows, :] = value
        m.yb[rows, :] = value.astype(BF16)

    looped(0, SUBS, child_y)
    for g in range(GROUPS):
        m.fac[g * RANK : (g + 1) * RANK, :] = dot(
            msk[:, g * BLK : (g + 1) * BLK], m.yb[g * BLK : (g + 1) * BLK, :]
        ).astype(BF16)
    route_rows(factors, dot(m.sel_s[...], m.fac[...]))

    v_start(parent, vp)
    for k in range(COLS):
        m.swap.src[k] = rp[:, k * NLOC : (k + 1) * NLOC].astype(BF16)
    m.swap.dst[c] = m.swap.src[c]
    col_send(m.swap)
    for n in range(COLS):
        load(parent, dp_hbm, n).wait()
    sum_away(parent.bsum, b_piece(parent))
    v_forward(parent)
    sum_here(parent.bsum, b_piece(parent))
    v_finish(parent)
    make_e(parent)
    kernel_send(parent, project(parent.ehl, parent.ut[...]), None)
    m.sel_r[...] = onehot((512, ROWS * 32), 1, src_col)
    weights.cols.src[...] = dot(m.sel_r[...], rows_of(weights)).astype(BF16).reshape(COLS, 128, BLK)
    route_cols(weights)
    _, transfer = kernel_sum(parent, pp)
    maps_send(parent, transfer, transfer.T)
    m.sel_rt[...] = onehot((ROWS * 32, 512), 0, src_row)
    m.sel_st[...] = onehot((512, ROWS * 32), 1, tgt_col)
    split_phi(child_back)
    m.mskt[...] = msk[...].astype(F32).T.astype(BF16)
    col_wait(m.swap)
    for k in range(SUBS):
        cols = slice(k * SUB, (k + 1) * SUB)
        m.rpt[cols, :] = m.swap.dst[:, :, cols].astype(F32).reshape(H, SUB).T
    b_finish(parent)
    row_wait(parent.maps)

    def parent_step(n, pair):
        rising, falling = pair
        j = ROWS - 1 - n
        store_phi(back, n, jnp.where(n > i, rising, 0.0))
        store_phi(ahead, j, jnp.where(j < i, falling, 0.0))
        up_next = jnp.dot(parent.maps.dst[n][:, :RANK], rising, precision=HIGH)
        down_next = jnp.dot(parent.maps.dst[j][:, RANK:], falling, precision=HIGH)
        return jnp.where(n > i, up_next, rising), jnp.where(j < i, down_next, falling)

    lax.fori_loop(0, ROWS, parent_step, (eye, eye))
    split_phi(ahead)
    split_phi(back)
    col_wait(weights.cols)

    factors.cols.src[...] = dot(m.sel_r[...], rows_of(factors)).astype(BF16).reshape(COLS, 128, H)
    route_cols(factors)
    col_wait(factors.cols)

    def joined(ref, q):
        return jnp.concatenate([ref[k, q * 16 : (q + 1) * 16, :] for k in range(COLS)], axis=0)

    for q in range(GROUPS):
        rows = slice(q * BLK, (q + 1) * BLK)
        contrib = dot_tn(joined(weights.cols.dst, q), joined(factors.cols.dst, q))
        m.rpb[rows, :] = (m.rpt[rows, :] - contrib).astype(BF16)

    scan_one(ahead, project(parent.ehl, m.rpb[...]))
    y_part = d_piece(parent, m.rpb)
    sum_away(parent.ysum, y_part)
    scan_two(ahead)
    sum_here(parent.ysum, y_part)
    scan_three(ahead)
    h_parent = wait_state(ahead.state)

    def parent_y(s):
        rows = pl.ds(pl.multiple_of(s * SUB, SUB), SUB)
        m.rpb[rows, :] = (sum_wait(parent.ysum, s) - dot(parent.bl[rows, :], h_parent)).astype(BF16)

    looped(0, SUBS, parent_y)
    z_start(parent, m.rpb)
    scan_one(back, project(parent.fhl, m.rpb[...]))
    z_apply(parent, c, xp_out, None)
    scan_two(back)
    z_apply(parent, peer, xp_out, 0)
    z_apply(parent, other, xp_out, 1)
    scan_three(back)
    z_apply(parent, diag, xp_out, 2)
    g_parent = wait_state(back.state)
    xp_out[...] -= dot_tn(g_parent, parent.ehl[:RANK])

    for q in range(GROUPS):
        values = dot_nt(joined(weights.cols.dst, q), xp_out[:, q * BLK : (q + 1) * BLK].astype(BF16)).astype(BF16)
        for k in range(COLS):
            pulled.cols.src[k, q * 16 : (q + 1) * 16, :] = values[k * 16 : (k + 1) * 16]
    route_cols(pulled)
    col_wait(pulled.cols)
    route_rows(pulled, dot(m.sel_rt[...], pulled.cols.dst[...].reshape(512, H)))
    m.fac[...] = dot(m.sel_st[...], rows_of(pulled)).astype(BF16)
    for g in range(GROUPS):
        rows = slice(g * BLK, (g + 1) * BLK)
        correction = dot(m.mskt[rows, :], m.fac[g * RANK : (g + 1) * RANK, :])
        m.yb[rows, :] = (m.y[rows, :] - correction).astype(BF16)

    z_start(child, m.yb)
    scan_one(child_back, project(child.fhl, m.yb[...]))
    z_apply(child, c, xc_out, None)
    scan_two(child_back)
    z_apply(child, peer, xc_out, 0)
    z_apply(child, other, xc_out, 1)
    scan_three(child_back)
    z_apply(child, diag, xc_out, 2)
    g_child = wait_state(child_back.state)
    xc_out[...] -= dot_tn(g_child, child.ehl[:RANK])
    for done in pending:
        done()


def shards(
    rhs_child, rhs_parent, dinv_child, dinv_parent, ubase_child, vbase_child, ubase_parent, vbase_parent,
    trans_child, trans_parent, w_first, w_second, block_ranks, extend_map,
):
    i = lax.axis_index("row")
    c = lax.axis_index("col")
    allowed = jnp.arange(RANK, dtype=jnp.int32)[:, None] < jnp.repeat(block_ranks, BLK)[None, :]
    masked = jnp.where(allowed, w_first, jnp.zeros_like(w_first))
    second = lax.dynamic_slice_in_dim(w_second, c * GROUPS, GROUPS, 0)
    second = second.reshape(GROUPS * RANK, BLK)

    entries = extend_map.reshape(ROWS, RANK)
    target = entries // 32
    serial = jnp.arange(RANK, dtype=jnp.int32)
    same = (target[:, :, None] == target[:, None, :]) & (serial[None, None, :] < serial[None, :, None])
    count = jnp.sum(same, axis=2, dtype=jnp.int32)
    groups = jnp.arange(GROUPS, dtype=jnp.int32) * SLOTS
    tgt = (lax.dynamic_index_in_dim(target * 32 + count, i, 0, False)[None, :] + groups[:, None]).reshape(-1)
    code = (jnp.arange(ROWS, dtype=jnp.int32)[:, None] * 32 + count).reshape(1, 2, -1)
    found = entries.reshape(1, 2, -1) == (i * 32 + jnp.arange(32, dtype=jnp.int32))[:, None, None]
    src = jnp.sum(jnp.where(found, code, 0), axis=2, dtype=jnp.int32)
    src = (src[:, :, None] + groups[None, None, :]).reshape(-1)

    vmem = pl.BlockSpec(memory_space=pltpu.VMEM)
    hbm = pl.BlockSpec(memory_space=pl.ANY)
    return tuple(
        pl.pallas_call(
            kernel,
            out_shape=[jax.ShapeDtypeStruct((H, NLOC), F32)] * 2,
            in_specs=[vmem, vmem, hbm, hbm] + [vmem] * 12,
            out_specs=[vmem, vmem],
            scratch_shapes=scratch_tree(),
            compiler_params=pltpu.CompilerParams(
                collective_id=0, has_side_effects=True, vmem_limit_bytes=60 * 1024 * 1024
            ),
        )(
            rhs_child,
            rhs_parent,
            dinv_child.reshape(COLS, NLOC, NLOC),
            dinv_parent.reshape(COLS, NLOC, NLOC),
            ubase_child,
            vbase_child,
            ubase_parent,
            vbase_parent,
            trans_child.reshape(RANK, RANK),
            trans_parent.reshape(RANK, RANK),
            masked,
            second,
            tgt[None, :],
            tgt[:, None],
            src[None, :],
            src[:, None],
        )
    )


def solution(mesh):
    return jax.shard_map(
        shards,
        mesh=mesh,
        in_specs=(
            P(None, ("row", "col")),
            P("col", "row"),
            P("row", "col"),
            P("row", "col"),
            P(None, ("row", "col")),
            P(None, ("row", "col")),
            P(None, ("row", "col")),
            P(None, ("row", "col")),
            P("row", None, None),
            P("row", None, None),
            P(None, ("row", "col")),
            P(None, "row"),
            P(("row", "col")),
            P(),
        ),
        out_specs=(P(None, ("row", "col")), P(None, ("row", "col"))),
        check_vma=False,
    )
```

```python
from typing import Any, NamedTuple

import jax
import jax.numpy as jnp
from jax import lax
from jax.experimental import pallas as pl
from jax.experimental.pallas import tpu as pltpu
from jax.sharding import PartitionSpec as P

MESH = pl.DeviceIdType.MESH
F32 = jnp.float32
BF16 = jnp.bfloat16
HIGH = lax.Precision.HIGHEST

ROWS = 32
COLS = 4
HALF = 16
H = 256
HS = 64
RANK = 64
NLOC = 1024
GROUPS = 8
BLK = 128
SUBS = 4
SUB = NLOC // SUBS
SLOTS = 4

DMA = pltpu.SemaphoreType.DMA


class Link(NamedTuple):
    src: Any
    dst: Any
    sent: Any
    came: Any


class Hops(NamedTuple):
    buf: Any
    sent: Any
    came: Any


class Sums(NamedTuple):
    a: Link
    b: Link


class Front(NamedTuple):
    d: Any
    loaded: Any
    ut: Any
    v: Hops
    e: Any
    ehl: Any
    fhl: Any
    bl: Any
    ysum: Sums
    bsum: Sums
    z: Hops
    kern: Link
    maps: Link


class Scan(NamedTuple):
    phi: Any
    phl: Any
    part: Link
    rows: Link
    state: Link


class Route(NamedTuple):
    rows: Link
    cols: Link


class Rest(NamedTuple):
    first: Link
    swap: Link
    sel_tall: Any
    sel_wide: Any
    held: Any
    acc: Any
    bacc: Any
    rt: Any
    rpt: Any
    rpb: Any
    y: Any
    yb: Any
    mskt: Any
    fac: Any
    msk: Any
    trans: Link
    rc: Any
    rp: Any
    w16: Any
    xp: Any
    near: Any


def link(src, dst, count, kind=BF16):
    source = None if src is None else pltpu.VMEM(src, kind)
    return Link(source, pltpu.VMEM(dst, kind), DMA((count,)), DMA((count,)))


def sums(subs, rows, lanes):
    two, one = (2 * subs, rows, lanes), (subs, rows, lanes)
    return Sums(link(two, two, 2 * subs), link(one, one, subs))


def front(count, tile):
    return Front(
        d=pltpu.VMEM((COLS, NLOC, NLOC), BF16),
        loaded=DMA((COLS,)),
        ut=pltpu.VMEM((NLOC, RANK), BF16),
        v=Hops(pltpu.VMEM((COLS, RANK, NLOC), BF16), DMA((3, 1)), DMA((3, 1))),
        e=pltpu.VMEM((RANK, NLOC), F32),
        ehl=pltpu.VMEM((2 * RANK, NLOC), BF16),
        fhl=pltpu.VMEM((2 * RANK, NLOC), BF16),
        bl=pltpu.VMEM((NLOC, RANK), BF16),
        ysum=sums(SUBS, SUB, H),
        bsum=sums(1, NLOC // 2, 2 * RANK),
        z=Hops(pltpu.VMEM((COLS, SUBS, H, SUB), BF16), DMA((3, SUBS)), DMA((3, SUBS))),
        kern=link((COLS, RANK, 2 * RANK), (2 * COLS, RANK, 2 * RANK), 2 * COLS),
        maps=link(None, (count // 2, 2) + tile, count // 2, F32),
    )


def scan(count):
    part = (RANK // 2, 2 * HS)
    return Scan(
        phi=pltpu.VMEM((count * RANK // 2, 2 * RANK), F32),
        phl=pltpu.VMEM((4 * RANK, count * RANK // 2), BF16),
        part=link((COLS,) + part, (2 * COLS,) + part, 2 * COLS),
        rows=link(None, (count // 2, 2) + part, count // 2),
        state=link(None, (COLS,) + part, COLS),
    )


def route(lanes):
    rows, cols = (ROWS, 32, lanes), (COLS, 128, lanes)
    return Route(link(rows, rows, ROWS), link(cols, cols, COLS))


def scratch_tree():
    part = (COLS, RANK // 2, 2 * HS)
    swap = (COLS, HS, NLOC)
    rest = Rest(
        first=link(None, part, COLS),
        swap=link(swap, swap, COLS),
        sel_tall=pltpu.VMEM((ROWS * 32, 512), BF16),
        sel_wide=pltpu.VMEM((512, ROWS * 32), BF16),
        held=pltpu.VMEM((SUBS, SUB, H), F32),
        acc=pltpu.VMEM((SUBS, SUB, H), F32),
        bacc=pltpu.VMEM((1, NLOC // 2, 2 * RANK), F32),
        rt=pltpu.VMEM((NLOC, H), BF16),
        rpt=pltpu.VMEM((NLOC, H), F32),
        rpb=pltpu.VMEM((NLOC, H), BF16),
        y=pltpu.VMEM((NLOC, H), F32),
        yb=pltpu.VMEM((NLOC, H), BF16),
        mskt=pltpu.VMEM((NLOC, RANK), BF16),
        fac=pltpu.VMEM((512, H), BF16),
        msk=pltpu.VMEM((RANK, NLOC), BF16),
        trans=link(None, (2, RANK, 2 * RANK), 1, F32),
        rc=pltpu.VMEM((H, NLOC), F32),
        rp=pltpu.VMEM((HS, COLS * NLOC), F32),
        w16=pltpu.VMEM((2 * GROUPS, RANK * BLK), BF16),
        xp=pltpu.VMEM((H, NLOC), F32),
        near=DMA((8,)),
    )
    return (
        front(HALF, (RANK, 2 * RANK)), front(ROWS, (RANK // 2, 2 * RANK)), scan(ROWS), scan(ROWS), scan(HALF), route(H), route(BLK), route(H), rest,
    )


def dot(a, b):
    return jnp.dot(a, b, preferred_element_type=F32)


def dot_tn(a, b):
    return lax.dot_general(a, b, (((0,), (0,)), ((), ())), preferred_element_type=F32)


def dot_nt(a, b):
    return lax.dot_general(a, b, (((1,), (1,)), ((), ())), preferred_element_type=F32)


def high_low(a):
    high = a.astype(BF16)
    return high, (a - high.astype(F32)).astype(BF16)


def kernel(
    rc_hbm, rp_hbm, dc_hbm, dp_hbm, w_hbm, uc, vc, up, vp, wf, pc, pp, entries, ranks,
    xc_out, xp_out, child, parent, ahead, back, child_back, factors, weights, pulled, m,
):
    i = lax.axis_index("row")
    c = lax.axis_index("col")
    peer = c + 1 - 2 * lax.rem(c, 2)
    other = lax.rem(c + 2, COLS)
    diag = lax.rem(peer + 2, COLS)
    loc = lax.rem(i, HALF)
    base = i - loc
    side = lax.rem(i, 2)
    twin = i + 1 - 2 * side
    dests = (diag, other, peer, c)
    pending = []

    def remote(src, dst, ss, rs, row, col):
        return pltpu.make_async_remote_copy(
            src_ref=src, dst_ref=dst, send_sem=ss, recv_sem=rs, device_id=(row, col), device_id_type=MESH
        )

    def looped(lo, hi, fn):
        def one(s, carry):
            fn(s)
            return carry

        lax.fori_loop(lo, hi, one, 0)

    def piece_of(ln, here, to):
        return ln.dst.at[here] if ln.src is None else ln.src.at[to]

    def col_copy(ln, d, to, slot):
        return remote(piece_of(ln, c, to), ln.dst.at[slot], ln.sent.at[d], ln.came.at[d], i, to)

    def col_send(ln):
        for d in range(1, COLS):
            col_copy(ln, d, lax.rem(c + d, COLS), c).start()
        pending.append(lambda: [col_copy(ln, d, lax.rem(c + d, COLS), c).wait_send() for d in range(1, COLS)])

    def col_wait(ln):
        for d in range(1, COLS):
            frm = lax.rem(c - d + COLS, COLS)
            col_copy(ln, d, frm, frm).wait_recv()

    def row_place(ln):
        n = ln.dst.shape[0]
        return (n, base, loc) if n == HALF else (n, 0, i)

    def row_copy(ln, d, to, slot):
        _, start, here = row_place(ln)
        return remote(piece_of(ln, here, to), ln.dst.at[slot], ln.sent.at[d], ln.came.at[d], start + to, c)

    def row_send(ln):
        n, _, here = row_place(ln)
        looped(1, n, lambda d: row_copy(ln, d, lax.rem(here + d, n), here).start())
        pending.append(
            lambda: looped(1, n, lambda d: row_copy(ln, d, lax.rem(here + d, n), here).wait_send())
        )

    def row_wait(ln):
        n, _, here = row_place(ln)

        def one(d):
            frm = lax.rem(here - d + n, n)
            row_copy(ln, d, frm, frm).wait_recv()

        looped(1, n, one)

    def twin_copy(ln, n, to, slot, row):
        return remote(ln.src.at[to], ln.dst.at[slot], ln.sent.at[n], ln.came.at[n], row, to)

    def twin_send(ln):
        for d in range(1, COLS):
            twin_copy(ln, d, lax.rem(c + d, COLS), side * COLS + c, i).start()
        for d in range(COLS):
            twin_copy(ln, COLS + d, lax.rem(c + d, COLS), side * COLS + c, twin).start()

        def done():
            for d in range(1, COLS):
                twin_copy(ln, d, lax.rem(c + d, COLS), side * COLS + c, i).wait_send()
            for d in range(COLS):
                twin_copy(ln, COLS + d, lax.rem(c + d, COLS), side * COLS + c, twin).wait_send()

        pending.append(done)

    def twin_wait(ln):
        ln.dst[side * COLS + c] = ln.src[c]
        for d in range(1, COLS):
            frm = lax.rem(c - d + COLS, COLS)
            twin_copy(ln, d, frm, side * COLS + frm, i).wait_recv()
        for d in range(COLS):
            frm = lax.rem(c - d + COLS, COLS)
            twin_copy(ln, COLS + d, frm, (1 - side) * COLS + frm, twin).wait_recv()
        return [jnp.sum(ln.dst[k * COLS : (k + 1) * COLS].astype(F32), axis=0) for k in range(2)]

    def pair_place(ln):
        n = ln.dst.shape[0]
        return (n, base, lax.div(loc, 2)) if n == HALF // 2 else (n, 0, lax.div(i, 2))

    def pair_copy(ln, d, to, slot):
        _, start, here = pair_place(ln)
        return remote(
            ln.dst.at[here], ln.dst.at[slot], ln.sent.at[d], ln.came.at[d], start + 2 * to + side, c
        )

    def pair_send(ln):
        n, _, here = pair_place(ln)
        looped(1, n, lambda d: pair_copy(ln, d, lax.rem(here + d, n), here).start())
        pending.append(
            lambda: looped(1, n, lambda d: pair_copy(ln, d, lax.rem(here + d, n), here).wait_send())
        )

    def pair_wait(ln):
        n, _, here = pair_place(ln)

        def one(d):
            frm = lax.rem(here - d + n, n)
            pair_copy(ln, d, frm, frm).wait_recv()

        looped(1, n, one)

    def hop(hops, step, s, whole=False):
        block = other if step == 2 else c
        to = other if step == 1 else peer
        ref = hops.buf.at[block] if whole else hops.buf.at[block, s]
        return remote(ref, ref, hops.sent.at[step, s], hops.came.at[step, s], i, to)

    def v_start(f, vbase):
        f.v.buf[c] = vbase[...]
        hop(f.v, 1, 0, True).start()
        hop(f.v, 0, 0, True).start()

    def v_forward(f):
        hop(f.v, 1, 0, True).wait_recv()
        hop(f.v, 2, 0, True).start()
        pending.append(lambda: [hop(f.v, step, 0, True).wait_send() for step in range(3)])

    def z_start(f, source):
        def one(s):
            piece = source[pl.ds(pl.multiple_of(s * SUB, SUB), SUB), :]
            f.z.buf[c, s] = piece.astype(F32).T.astype(BF16)
            hop(f.z, 0, s).start()

        def first(s):
            one(s)
            hop(f.z, 1, s).start()

        looped(0, SUBS - 1, first)
        one(SUBS - 1)

        def each(s):
            for step in range(3):
                hop(f.z, step, s).wait_send()

        pending.append(lambda: looped(0, SUBS, each))

    def z_apply(f, block, out, step):
        def one(s):
            if step is not None:
                hop(f.z, step, s).wait_recv()
                if step == 1:
                    hop(f.z, 2, s).start()
            out[...] += dot(f.z.buf[block, s], f.d[block, pl.ds(pl.multiple_of(s * SUB, SUB), SUB), :])

        if step is None:
            out[...] = jnp.zeros(out.shape, F32)
        looped(0, SUBS, one)

    def within(sm, n):
        return remote(sm.a.src.at[n], sm.a.dst.at[n], sm.a.sent.at[n], sm.a.came.at[n], i, peer)

    def between(sm, n):
        return remote(sm.b.src.at[n], sm.b.dst.at[n], sm.b.sent.at[n], sm.b.came.at[n], i, other)

    def a_pieces(sm, n, dest, piece):
        subs = sm.b.dst.shape[0]

        def one(p):
            out = piece(dest, p).astype(BF16)
            if subs == 1:
                sm.a.src[n] = out
            else:
                sm.a.src[n * subs + 2 * p] = out[:SUB]
                sm.a.src[n * subs + 2 * p + 1] = out[SUB:]

        looped(0, max(subs // 2, 1), one)

    def a_send(sm, n):
        subs = sm.b.dst.shape[0]
        looped(0, subs, lambda s: within(sm, n * subs + s).start())

    def own_pieces(sm, into, dest, piece):
        subs = sm.b.dst.shape[0]

        def one(p):
            out = piece(dest, p)
            if subs == 1:
                into[0] = out
            else:
                into[2 * p] = out[:SUB]
                into[2 * p + 1] = out[SUB:]

        looped(0, max(subs // 2, 1), one)

    def b_make(sm, held):
        def one(s):
            within(sm, s).wait_recv()
            sm.b.src[s] = (held[s] + sm.a.dst[s].astype(F32)).astype(BF16)

        looped(0, sm.b.dst.shape[0], one)

    def b_send(sm, lo, hi):
        looped(lo, hi, lambda s: between(sm, s).start())
        if hi == sm.b.dst.shape[0]:
            subs = hi

            def each(s):
                within(sm, s).wait_send()
                within(sm, subs + s).wait_send()
                between(sm, s).wait_send()

            pending.append(lambda: looped(0, subs, each))

    def b_sums(f):
        piece = b_piece(f)
        a_pieces(f.bsum, 0, diag, piece)
        a_send(f.bsum, 0)
        a_pieces(f.bsum, 1, peer, piece)
        a_send(f.bsum, 1)
        own_pieces(f.bsum, m.bacc, other, piece)
        b_make(f.bsum, m.bacc)
        b_send(f.bsum, 0, 1)
        own_pieces(f.bsum, m.bacc, c, piece)

    def sum_wait(sm, s):
        subs = sm.b.dst.shape[0]
        within(sm, subs + s).wait_recv()
        between(sm, s).wait_recv()
        acc = m.bacc if subs == 1 else m.acc
        return acc[s] + sm.a.dst[subs + s].astype(F32) + sm.b.dst[s].astype(F32)

    def d_piece(f, rhs):
        def piece(dest, s):
            return dot(f.d[dest, pl.ds(pl.multiple_of(s * 2 * SUB, 2 * SUB), 2 * SUB), :], rhs[...])

        return piece

    def b_piece(f):
        def piece(dest, s):
            out = dot(f.d[dest], f.ut[...])
            return jnp.concatenate([out[: NLOC // 2], out[NLOC // 2 :]], axis=1)

        return piece

    def b_finish(f):
        packed = sum_wait(f.bsum, 0)
        out = jnp.concatenate([packed[:, :RANK], packed[:, RANK:]], axis=0)
        f.bl[...] = out.astype(BF16)
        high, low = high_low(out.T)
        f.fhl[:RANK] = high
        f.fhl[RANK:] = low

    def make_e(f):
        def add(block):
            f.e[...] += dot(f.v.buf[block], f.d[block])

        f.e[...] = dot(f.v.buf[c], f.d[c])
        v_forward(f)
        add(other)
        hop(f.v, 0, 0, True).wait_recv()
        add(peer)
        hop(f.v, 2, 0, True).wait_recv()
        add(diag)
        high, low = high_low(f.e[...])
        f.ehl[:RANK] = high
        f.ehl[RANK:] = low

    def project(pair, vec):
        both = dot(pair[...], vec)
        return both[:RANK] + both[RANK:]

    def pack(a):
        return jnp.concatenate([a[: RANK // 2], a[RANK // 2 :]], axis=1)

    def unpack(a):
        return jnp.concatenate([a[:, :HS], a[:, HS:]], axis=0)

    def scan_one(sc, partial):
        for k in range(COLS):
            sc.part.src[k] = pack(partial[:, k * HS : (k + 1) * HS]).astype(BF16)
        twin_send(sc.part)

    def scan_two(sc):
        here = pair_place(sc.rows)[2]
        for k, total in enumerate(twin_wait(sc.part)):
            sc.rows.dst[here, k] = total.astype(BF16)
        pair_send(sc.rows)

    def scan_three(sc):
        pair_wait(sc.rows)
        both = dot(sc.phl[...], sc.rows.dst[...].reshape(sc.phl.shape[1], 2 * HS))
        both = both[: 2 * RANK] + both[2 * RANK :]
        send_state(sc.state, both[:RANK, :HS] + both[RANK:, HS:])

    def send_state(ln, state):
        ln.dst[c] = pack(state).astype(BF16)
        col_send(ln)

    def wait_state(ln):
        col_wait(ln)
        return jnp.concatenate([unpack(ln.dst[k].astype(F32)) for k in range(COLS)], axis=1).astype(BF16)

    def split_phi(sc):
        high, low = high_low(sc.phi[...].T)
        sc.phl[: 2 * RANK] = high
        sc.phl[2 * RANK :] = low

    def kernel_send(f, kernel_part, source):
        for k in range(COLS):
            left = kernel_part if source is None else source[:, k * HS : (k + 1) * HS]
            f.kern.src[k] = jnp.concatenate([left, kernel_part], axis=1).astype(BF16)
        twin_send(f.kern)

    def route_values(rt, values):
        rt.rows.src[...] = values.astype(BF16).reshape(rt.rows.src.shape)
        rt.rows.dst[i] = rt.rows.src[i]

    def route_rows(rt, values):
        route_values(rt, values)
        row_send(rt.rows)

    def route_cols(rt):
        rt.cols.dst[c] = rt.cols.src[c]
        col_send(rt.cols)

    def rows_of(rt):
        row_wait(rt.rows)
        return rt.rows.dst[...].reshape(ROWS * 32, rt.rows.dst.shape[2])

    def onehot(shape, axis, at):
        return (lax.broadcasted_iota(jnp.int32, shape, axis) == at).astype(BF16)

    def load(f, hbm, n):
        return pltpu.make_async_copy(hbm.at[dests[n]], f.d.at[dests[n]], f.loaded.at[n])

    load_rc = pltpu.make_async_copy(rc_hbm, m.rc, m.near.at[0])
    load_rp = pltpu.make_async_copy(rp_hbm, m.rp, m.near.at[1])
    load_w = pltpu.make_async_copy(
        w_hbm.at[pl.ds(pl.multiple_of(lax.div(c, 2) * 2 * GROUPS, 2 * GROUPS), 2 * GROUPS), :], m.w16, m.near.at[2]
    )
    load_rc.start()
    for n in range(COLS):
        load(child, dc_hbm, n).start()
    for n in range(COLS):
        load(parent, dp_hbm, n).start()
    load_w.start()
    load_rp.start()

    barrier = pltpu.get_barrier_semaphore()

    def greet(row, col):
        pl.semaphore_signal(barrier, inc=1, device_id=(row, col), device_id_type=MESH)

    looped(1, ROWS, lambda d: greet(lax.rem(i + d, ROWS), c))
    for d in range(1, COLS):
        greet(i, lax.rem(c + d, COLS))
        greet(twin, lax.rem(c + d, COLS))

    child.ut[...] = uc[...].astype(F32).T.astype(BF16)
    parent.ut[...] = up[...].astype(F32).T.astype(BF16)
    load_rc.wait()
    for s in range(SUBS):
        m.rt[s * SUB : (s + 1) * SUB, :] = m.rc[:, s * SUB : (s + 1) * SUB].T.astype(BF16)
    y_part = d_piece(child, m.rt)
    load(child, dc_hbm, 0).wait()
    a_pieces(child.ysum, 0, diag, y_part)
    load(child, dc_hbm, 1).wait()
    own_pieces(child.ysum, m.held, other, y_part)
    m.trans.dst[side] = jnp.concatenate([pc[...], pp[...]], axis=1)
    pl.semaphore_wait(barrier, ROWS - 1 + 2 * (COLS - 1))

    v_start(child, vc)
    v_start(parent, vp)
    trans_copy = remote(
        m.trans.dst.at[side], m.trans.dst.at[side], m.trans.sent.at[0], m.trans.came.at[0], twin, c
    )
    trans_from = remote(
        m.trans.dst.at[1 - side], m.trans.dst.at[1 - side], m.trans.sent.at[0], m.trans.came.at[0], twin, c
    )
    trans_copy.start()
    pending.append(trans_copy.wait_send)
    a_send(child.ysum, 0)
    load(child, dc_hbm, 2).wait()
    load(child, dc_hbm, 3).wait()
    make_e(child)
    kernel_send(child, project(child.ehl, child.ut[...]), project(child.ehl, m.rt[...]))
    a_pieces(child.ysum, 1, peer, y_part)
    a_send(child.ysum, 1)
    own_pieces(child.ysum, m.acc, c, y_part)
    b_make(child.ysum, m.held)
    trans_from.wait_recv()
    here = pair_place(child.maps)[2]
    for k, total in enumerate(twin_wait(child.kern)):
        transfer = m.trans.dst[k, :, :RANK] - total[:, RANK:]
        child.maps.dst[here, k] = jnp.concatenate([transfer, total[:, :RANK]], axis=1)
    pair_send(child.maps)
    b_send(child.ysum, 0, SUBS - 1)
    for n in range(COLS):
        load(parent, dp_hbm, n).wait()
    make_e(parent)
    kernel_send(parent, project(parent.ehl, parent.ut[...]), None)
    b_send(child.ysum, SUBS - 1, SUBS)
    b_sums(child)

    eye = (
        lax.broadcasted_iota(jnp.int32, (RANK, RANK), 0) == lax.broadcasted_iota(jnp.int32, (RANK, RANK), 1)
    )
    eye_f = eye.astype(F32)
    left = lax.broadcasted_iota(jnp.int32, (RANK, 2 * RANK), 1) < RANK

    def iota(rows, cols, axis):
        return lax.broadcasted_iota(jnp.int32, (rows, cols), axis)

    def over_lanes(mask, values):
        return jnp.sum(jnp.where(mask, values, 0), axis=1, keepdims=True)

    def over_rows(mask, values):
        return jnp.sum(jnp.where(mask, values, 0), axis=0, keepdims=True)

    mine = entries[pl.ds(i, 1), :] >> 5
    mine_col = over_lanes(eye, mine)
    earlier = (mine_col == mine) & (iota(RANK, RANK, 1) < iota(RANK, RANK, 0))
    tgt_col = mine_col * 32 + jnp.sum(earlier.astype(jnp.int32), axis=1, keepdims=True)
    tgt_row = over_rows(eye, tgt_col)
    wide = iota(RANK, 512, 1)
    tall = iota(512, RANK, 0)
    by_group = over_rows(iota(RANK, 512, 0) == (wide & (RANK - 1)), tgt_col) + 4 * (iota(1, 512, 1) >> 6)
    by_block = over_rows(iota(RANK, 512, 0) == (wide >> 3), tgt_col) + 4 * (iota(1, 512, 1) & 7)
    m.sel_tall[...] = onehot((ROWS * 32, 512), 0, by_block)
    load_w.wait()
    w16 = m.w16[...].astype(F32)
    w8 = jnp.where(lax.rem(c, 2) == 0, w16[:GROUPS], w16[GROUPS:])
    ws = jnp.concatenate([w8[:, b * BLK : (b + 1) * BLK] for b in range(RANK)], axis=0).astype(BF16)
    route_values(weights, dot(m.sel_tall[...], ws))
    m.sel_tall[...] = onehot((ROWS * 32, 512), 0, by_group)
    for g in range(GROUPS):
        cols = slice(g * BLK, (g + 1) * BLK)
        allowed = iota(RANK, BLK, 0) < ranks[g]
        m.msk[:, cols] = jnp.where(allowed, wf[:, cols].astype(F32), 0.0).astype(BF16)

    here = pair_place(parent.maps)[2]
    for k, total in enumerate(twin_wait(parent.kern)):
        parent.maps.dst[here, k] = pack(m.trans.dst[k, :, RANK:] - total[:, RANK:])
    pair_send(parent.maps)
    pair_wait(child.maps)
    row_send(weights.rows)

    def store_phi(sc, j, value):
        sc.phi[pl.ds(pl.multiple_of(j * (RANK // 2), RANK // 2), RANK // 2), :] = pack(value)

    def child_step(j, both):
        now = child.maps.dst[lax.div(j, 2), lax.rem(j, 2)]
        product = jnp.dot(now[:, :RANK], both, precision=HIGH)
        added = jnp.concatenate([now[:, RANK:], jnp.zeros((RANK, RANK), F32)], axis=1)
        store_phi(child_back, j, jnp.where(j > loc, both[:, RANK:], 0.0))
        moves = (left & (j < loc)) | (~left & (j > loc))
        return jnp.where(moves, product + added, both)

    both = lax.fori_loop(
        0, HALF, child_step, jnp.concatenate([jnp.zeros((RANK, RANK), F32), eye_f], axis=1)
    )
    send_state(m.first, both[:, :RANK])
    b_finish(child)
    h_child = wait_state(m.first)

    def child_y(s):
        rows = pl.ds(pl.multiple_of(s * SUB, SUB), SUB)
        value = sum_wait(child.ysum, s) - dot(child.bl[rows, :], h_child)
        m.y[rows, :] = value
        m.yb[rows, :] = value.astype(BF16)

    looped(0, SUBS, child_y)
    for g in range(GROUPS):
        m.fac[g * RANK : (g + 1) * RANK, :] = dot(
            m.msk[:, g * BLK : (g + 1) * BLK], m.yb[g * BLK : (g + 1) * BLK, :]
        ).astype(BF16)
    route_rows(factors, dot(m.sel_tall[...], m.fac[...]))

    load_rp.wait()
    for k in range(COLS):
        m.swap.src[k] = m.rp[:, k * NLOC : (k + 1) * NLOC].astype(BF16)
    m.swap.dst[c] = m.swap.src[c]
    col_send(m.swap)
    b_sums(parent)

    held_here = ((entries[...] >> 5) == i).astype(BF16)
    below = (iota(RANK, RANK, 0) < iota(RANK, RANK, 1)).astype(BF16)
    code = dot(held_here, below).astype(jnp.int32) + 32 * iota(ROWS, RANK, 0)
    wanted = i * 32 + (iota(RANK, RANK, 0) >> 1)
    second_half = iota(RANK, RANK, 0) & 1
    found = jnp.zeros((RANK, RANK), jnp.int32)
    for j in range(ROWS):
        hit = (entries[j : j + 1, :] == wanted) & (second_half == j // HALF)
        found = found + jnp.where(hit, code[j : j + 1, :], 0)
    src_col = jnp.sum(found, axis=1, keepdims=True)
    src_row = over_rows(eye, src_col)
    src_tall = over_lanes(iota(512, RANK, 1) == (tall >> 3), src_row) + 4 * (iota(512, 1, 0) & 7)
    src_wide = over_rows(iota(RANK, 512, 0) == (wide >> 3), src_col) + 4 * (iota(1, 512, 1) & 7)
    tgt_tall = over_lanes(iota(512, RANK, 1) == (tall & (RANK - 1)), tgt_row) + 4 * (iota(512, 1, 0) >> 6)
    m.sel_wide[...] = onehot((512, ROWS * 32), 1, src_tall)
    weights.cols.src[...] = dot(m.sel_wide[...], rows_of(weights)).astype(BF16).reshape(COLS, 128, BLK)
    route_cols(weights)
    pair_wait(parent.maps)

    def parent_step(n, pair):
        rising, falling = pair
        j = ROWS - 1 - n
        store_phi(back, n, jnp.where(n > i, rising, 0.0))
        store_phi(ahead, j, jnp.where(j < i, falling, 0.0).T)
        up_next = jnp.dot(unpack(parent.maps.dst[lax.div(n, 2), lax.rem(n, 2)]), rising, precision=HIGH)
        down_next = jnp.dot(falling, unpack(parent.maps.dst[lax.div(j, 2), lax.rem(j, 2)]), precision=HIGH)
        return jnp.where(n > i, up_next, rising), jnp.where(j < i, down_next, falling)

    lax.fori_loop(0, ROWS, parent_step, (eye_f, eye_f))
    split_phi(ahead)
    split_phi(back)
    split_phi(child_back)
    col_wait(m.swap)
    for k in range(SUBS):
        cols = slice(k * SUB, (k + 1) * SUB)
        m.rpt[cols, :] = m.swap.dst[:, :, cols].astype(F32).reshape(H, SUB).T
    b_finish(parent)
    col_wait(weights.cols)

    factors.cols.src[...] = dot(m.sel_wide[...], rows_of(factors)).astype(BF16).reshape(COLS, 128, H)
    route_cols(factors)
    m.mskt[...] = m.msk[...].astype(F32).T.astype(BF16)
    m.sel_tall[...] = onehot((ROWS * 32, 512), 0, src_wide)
    m.sel_wide[...] = onehot((512, ROWS * 32), 1, tgt_tall)
    col_wait(factors.cols)

    def joined(ref, q):
        return jnp.concatenate([ref[k, q * 16 : (q + 1) * 16, :] for k in range(COLS)], axis=0)

    for q in range(GROUPS):
        rows = slice(q * BLK, (q + 1) * BLK)
        contrib = dot_tn(joined(weights.cols.dst, q), joined(factors.cols.dst, q))
        m.rpb[rows, :] = (m.rpt[rows, :] - contrib).astype(BF16)

    scan_one(ahead, project(parent.ehl, m.rpb[...]))
    y_part = d_piece(parent, m.rpb)
    a_pieces(parent.ysum, 0, diag, y_part)
    a_send(parent.ysum, 0)
    own_pieces(parent.ysum, m.held, other, y_part)
    b_make(parent.ysum, m.held)
    b_send(parent.ysum, 0, SUBS - 1)
    scan_two(ahead)
    a_pieces(parent.ysum, 1, peer, y_part)
    a_send(parent.ysum, 1)
    own_pieces(parent.ysum, m.acc, c, y_part)
    scan_three(ahead)
    b_send(parent.ysum, SUBS - 1, SUBS)
    h_parent = wait_state(ahead.state)

    def parent_y(s):
        rows = pl.ds(pl.multiple_of(s * SUB, SUB), SUB)
        m.rpb[rows, :] = (sum_wait(parent.ysum, s) - dot(parent.bl[rows, :], h_parent)).astype(BF16)

    looped(0, SUBS, parent_y)
    scan_one(back, project(parent.fhl, m.rpb[...]))
    z_start(parent, m.rpb)
    z_apply(parent, c, m.xp, None)
    scan_two(back)
    z_apply(parent, peer, m.xp, 0)
    scan_three(back)
    hop(parent.z, 1, SUBS - 1).start()
    z_apply(parent, other, m.xp, 1)
    z_apply(parent, diag, m.xp, 2)
    g_parent = wait_state(back.state)
    m.xp[...] -= dot_tn(g_parent, parent.ehl[:RANK])
    store_xp = pltpu.make_async_copy(m.xp, xp_out, m.near.at[3])
    store_xp.start()
    pending.append(store_xp.wait)

    for q in range(GROUPS):
        values = dot_nt(joined(weights.cols.dst, q), m.xp[:, q * BLK : (q + 1) * BLK].astype(BF16)).astype(BF16)
        for k in range(COLS):
            pulled.cols.src[k, q * 16 : (q + 1) * 16, :] = values[k * 16 : (k + 1) * 16]
    route_cols(pulled)
    col_wait(pulled.cols)
    route_rows(pulled, dot(m.sel_tall[...], pulled.cols.dst[...].reshape(512, H)))
    m.fac[...] = dot(m.sel_wide[...], rows_of(pulled)).astype(BF16)
    for g in range(GROUPS):
        rows = slice(g * BLK, (g + 1) * BLK)
        correction = dot(m.mskt[rows, :], m.fac[g * RANK : (g + 1) * RANK, :])
        m.yb[rows, :] = (m.y[rows, :] - correction).astype(BF16)

    scan_one(child_back, project(child.fhl, m.yb[...]))
    z_start(child, m.yb)
    z_apply(child, c, m.rc, None)
    scan_two(child_back)
    z_apply(child, peer, m.rc, 0)
    scan_three(child_back)
    hop(child.z, 1, SUBS - 1).start()
    z_apply(child, other, m.rc, 1)
    z_apply(child, diag, m.rc, 2)
    g_child = wait_state(child_back.state)
    m.rc[...] -= dot_tn(g_child, child.ehl[:RANK])
    store_xc = pltpu.make_async_copy(m.rc, xc_out, m.near.at[4])
    store_xc.start()
    pending.append(store_xc.wait)
    for done in pending:
        done()


def hand_over(xc, xp, xc_out, xp_out):
    xc_out[...] = xc[...]
    xp_out[...] = xp[...]


def shards(
    rhs_child, rhs_parent, dinv_child, dinv_parent, ubase_child, vbase_child, ubase_parent, vbase_parent,
    trans_child, trans_parent, w_first, w_second, block_ranks, extend_map,
):
    vmem = pl.BlockSpec(memory_space=pltpu.VMEM)
    hbm = pl.BlockSpec(memory_space=pl.ANY)
    smem = pl.BlockSpec(memory_space=pltpu.SMEM)
    shapes = [jax.ShapeDtypeStruct((H, NLOC), F32)] * 2
    x_child, x_parent = pl.pallas_call(
        kernel,
        out_shape=shapes,
        in_specs=[hbm] * 5 + [vmem] * 8 + [smem],
        out_specs=[hbm, hbm],
        scratch_shapes=scratch_tree(),
        compiler_params=pltpu.CompilerParams(
            collective_id=0, has_side_effects=True, vmem_limit_bytes=60 * 1024 * 1024
        ),
    )(
        rhs_child,
        rhs_parent,
        dinv_child.reshape(COLS, NLOC, NLOC),
        dinv_parent.reshape(COLS, NLOC, NLOC),
        w_second,
        ubase_child,
        vbase_child,
        ubase_parent,
        vbase_parent,
        w_first,
        trans_child.reshape(RANK, RANK),
        trans_parent.reshape(RANK, RANK),
        extend_map.reshape(ROWS, RANK),
        block_ranks,
    )
    tile = pl.BlockSpec((H // 4, NLOC), lambda n: (n, 0))
    return tuple(
        pl.pallas_call(
            hand_over,
            grid=(4,),
            out_shape=shapes,
            in_specs=[tile, tile],
            out_specs=[tile, tile],
        )(x_child, x_parent)
    )


def solution(mesh):
    return jax.shard_map(
        shards,
        mesh=mesh,
        in_specs=(
            P(None, ("row", "col")),
            P("col", "row"),
            P("row", "col"),
            P("row", "col"),
            P(None, ("row", "col")),
            P(None, ("row", "col")),
            P(None, ("row", "col")),
            P(None, ("row", "col")),
            P("row", None, None),
            P("row", None, None),
            P(None, ("row", "col")),
            P(None, "row"),
            P(("row", "col")),
            P(),
        ),
        out_specs=(P(None, ("row", "col")), P(None, ("row", "col"))),
        check_vma=False,
    )
```

```python
from typing import Any, NamedTuple

import jax
import jax.numpy as jnp
from jax import lax
from jax.experimental import pallas as pl
from jax.experimental.pallas import tpu as pltpu
from jax.sharding import PartitionSpec as P

MESH = pl.DeviceIdType.MESH
F32 = jnp.float32
BF16 = jnp.bfloat16
HIGH = lax.Precision.HIGHEST

ROWS = 32
COLS = 4
HALF = 16
H = 256
HS = 64
RANK = 64
NLOC = 1024
GROUPS = 8
BLK = 128
SUBS = 4
SUB = NLOC // SUBS
SLOTS = 4

DMA = pltpu.SemaphoreType.DMA


class Link(NamedTuple):
    src: Any
    dst: Any
    sent: Any
    came: Any


class Hops(NamedTuple):
    buf: Any
    sent: Any
    came: Any


class Sums(NamedTuple):
    a: Link
    b: Link


class Front(NamedTuple):
    d: Any
    loaded: Any
    ut: Any
    v: Hops
    e: Any
    ehl: Any
    fhl: Any
    bl: Any
    ysum: Sums
    bsum: Sums
    z: Hops
    kern: Link
    maps: Link


class Scan(NamedTuple):
    phi: Any
    phl: Any
    part: Link
    rows: Link
    state: Link


class Route(NamedTuple):
    rows: Link
    cols: Link


class Rest(NamedTuple):
    first: Link
    swap: Link
    sel_tall: Any
    sel_wide: Any
    acc: Any
    bacc: Any
    rt: Any
    rpt: Any
    rpb: Any
    y: Any
    yb: Any
    mskt: Any
    fac: Any
    msk: Any
    trans: Link
    rc: Any
    rp: Any
    w16: Any
    xp: Any
    near: Any


def link(src, dst, count, kind=BF16):
    source = None if src is None else pltpu.VMEM(src, kind)
    return Link(source, pltpu.VMEM(dst, kind), DMA((count,)), DMA((count,)))


def sums(subs, rows, lanes):
    two, one = (2 * subs, rows, lanes), (subs, rows, lanes)
    return Sums(link(two, two, 2 * subs), link(one, one, subs))


def front(count, tile):
    return Front(
        d=pltpu.VMEM((COLS, NLOC, NLOC), BF16),
        loaded=DMA((COLS,)),
        ut=pltpu.VMEM((NLOC, RANK), BF16),
        v=Hops(pltpu.VMEM((COLS, RANK, NLOC), BF16), DMA((3, 1)), DMA((3, 1))),
        e=pltpu.VMEM((RANK, NLOC), F32),
        ehl=pltpu.VMEM((2 * RANK, NLOC), BF16),
        fhl=pltpu.VMEM((2 * RANK, NLOC), BF16),
        bl=pltpu.VMEM((NLOC, RANK), BF16),
        ysum=sums(SUBS, SUB, H),
        bsum=sums(1, NLOC // 2, 2 * RANK),
        z=Hops(pltpu.VMEM((COLS, SUBS, H, SUB), BF16), DMA((3, SUBS)), DMA((3, SUBS))),
        kern=link((COLS,) + tile, (2 * COLS,) + tile, 2 * COLS),
        maps=link(None, (count // 2, 2) + tile, count // 2, F32),
    )


def scan(count):
    part = (RANK // 2, 2 * HS)
    return Scan(
        phi=pltpu.VMEM((count * RANK // 2, 2 * RANK), F32),
        phl=pltpu.VMEM((4 * RANK, count * RANK // 2), BF16),
        part=link((COLS,) + part, (2 * COLS,) + part, 2 * COLS),
        rows=link(None, (count // 2, 2) + part, count // 2),
        state=link(None, (COLS,) + part, COLS),
    )


def route(lanes):
    rows, cols = (ROWS, 32, lanes), (COLS, 128, lanes)
    return Route(link(rows, rows, ROWS), link(cols, cols, COLS))


def scratch_tree():
    part = (COLS, RANK // 2, 2 * HS)
    swap = (COLS, HS, NLOC)
    rest = Rest(
        first=link(None, part, COLS),
        swap=link(swap, swap, COLS),
        sel_tall=pltpu.VMEM((ROWS * 32, 512), BF16),
        sel_wide=pltpu.VMEM((512, ROWS * 32), BF16),
        acc=pltpu.VMEM((SUBS, SUB, H), F32),
        bacc=pltpu.VMEM((2, 1, NLOC // 2, 2 * RANK), F32),
        rt=pltpu.VMEM((NLOC, H), BF16),
        rpt=pltpu.VMEM((NLOC, H), F32),
        rpb=pltpu.VMEM((NLOC, H), BF16),
        y=pltpu.VMEM((NLOC, H), F32),
        yb=pltpu.VMEM((NLOC, H), BF16),
        mskt=pltpu.VMEM((NLOC, RANK), BF16),
        fac=pltpu.VMEM((512, H), BF16),
        msk=pltpu.VMEM((RANK, NLOC), BF16),
        trans=link(None, (2, RANK, 2 * RANK), 1, F32),
        rc=pltpu.VMEM((H, NLOC), F32),
        rp=pltpu.VMEM((HS, COLS * NLOC), F32),
        w16=pltpu.VMEM((2 * GROUPS, RANK * BLK), BF16),
        xp=pltpu.VMEM((H, NLOC), F32),
        near=DMA((8,)),
    )
    return (
        front(HALF, (RANK, 2 * RANK)), front(ROWS, (RANK // 2, 2 * RANK)), scan(ROWS), scan(ROWS), scan(HALF), route(H), route(BLK), route(H), rest,
    )


def dot(a, b):
    return jnp.dot(a, b, preferred_element_type=F32)


def dot_tn(a, b):
    return lax.dot_general(a, b, (((0,), (0,)), ((), ())), preferred_element_type=F32)


def dot_nt(a, b):
    return lax.dot_general(a, b, (((1,), (1,)), ((), ())), preferred_element_type=F32)


def high_low(a):
    high = a.astype(BF16)
    return high, (a - high.astype(F32)).astype(BF16)


def kernel(
    rc_hbm, rp_hbm, dc_hbm, dp_hbm, w_hbm, uc, vc, up, vp, wf, pc, pp, entries, ranks,
    xc_out, xp_out, child, parent, ahead, back, child_back, factors, weights, pulled, m,
):
    i = lax.axis_index("row")
    c = lax.axis_index("col")
    peer = c + 1 - 2 * lax.rem(c, 2)
    other = lax.rem(c + 2, COLS)
    diag = lax.rem(peer + 2, COLS)
    loc = lax.rem(i, HALF)
    base = i - loc
    side = lax.rem(i, 2)
    twin = i + 1 - 2 * side
    dests = (diag, other, peer, c)
    pending = []

    def remote(src, dst, ss, rs, row, col):
        return pltpu.make_async_remote_copy(
            src_ref=src, dst_ref=dst, send_sem=ss, recv_sem=rs, device_id=(row, col), device_id_type=MESH
        )

    def looped(lo, hi, fn):
        def one(s, carry):
            fn(s)
            return carry

        lax.fori_loop(lo, hi, one, 0)

    def piece_of(ln, here, to):
        return ln.dst.at[here] if ln.src is None else ln.src.at[to]

    def col_copy(ln, d, to, slot):
        return remote(piece_of(ln, c, to), ln.dst.at[slot], ln.sent.at[d], ln.came.at[d], i, to)

    def col_send(ln):
        for d in range(1, COLS):
            col_copy(ln, d, lax.rem(c + d, COLS), c).start()
        pending.append(lambda: [col_copy(ln, d, lax.rem(c + d, COLS), c).wait_send() for d in range(1, COLS)])

    def col_wait(ln):
        for d in range(1, COLS):
            frm = lax.rem(c - d + COLS, COLS)
            col_copy(ln, d, frm, frm).wait_recv()

    def row_place(ln):
        n = ln.dst.shape[0]
        return (n, base, loc) if n == HALF else (n, 0, i)

    def row_copy(ln, d, to, slot):
        _, start, here = row_place(ln)
        return remote(piece_of(ln, here, to), ln.dst.at[slot], ln.sent.at[d], ln.came.at[d], start + to, c)

    def row_send(ln):
        n, _, here = row_place(ln)
        looped(1, n, lambda d: row_copy(ln, d, lax.rem(here + d, n), here).start())
        pending.append(
            lambda: looped(1, n, lambda d: row_copy(ln, d, lax.rem(here + d, n), here).wait_send())
        )

    def row_wait(ln):
        n, _, here = row_place(ln)

        def one(d):
            frm = lax.rem(here - d + n, n)
            row_copy(ln, d, frm, frm).wait_recv()

        looped(1, n, one)

    def twin_copy(ln, n, to, slot, row):
        return remote(ln.src.at[to], ln.dst.at[slot], ln.sent.at[n], ln.came.at[n], row, to)

    def twin_send(ln):
        for d in range(1, COLS):
            twin_copy(ln, d, lax.rem(c + d, COLS), side * COLS + c, i).start()
        for d in range(COLS):
            twin_copy(ln, COLS + d, lax.rem(c + d, COLS), side * COLS + c, twin).start()

        def done():
            for d in range(1, COLS):
                twin_copy(ln, d, lax.rem(c + d, COLS), side * COLS + c, i).wait_send()
            for d in range(COLS):
                twin_copy(ln, COLS + d, lax.rem(c + d, COLS), side * COLS + c, twin).wait_send()

        pending.append(done)

    def twin_wait(ln):
        ln.dst[side * COLS + c] = ln.src[c]
        for d in range(1, COLS):
            frm = lax.rem(c - d + COLS, COLS)
            twin_copy(ln, d, frm, side * COLS + frm, i).wait_recv()
        for d in range(COLS):
            frm = lax.rem(c - d + COLS, COLS)
            twin_copy(ln, COLS + d, frm, (1 - side) * COLS + frm, twin).wait_recv()
        return [jnp.sum(ln.dst[k * COLS : (k + 1) * COLS].astype(F32), axis=0) for k in range(2)]

    def pair_place(ln):
        n = ln.dst.shape[0]
        return (n, base, lax.div(loc, 2)) if n == HALF // 2 else (n, 0, lax.div(i, 2))

    def pair_copy(ln, d, to, slot):
        _, start, here = pair_place(ln)
        return remote(
            ln.dst.at[here], ln.dst.at[slot], ln.sent.at[d], ln.came.at[d], start + 2 * to + side, c
        )

    def pair_send(ln):
        n, _, here = pair_place(ln)
        looped(1, n, lambda d: pair_copy(ln, d, lax.rem(here + d, n), here).start())
        pending.append(
            lambda: looped(1, n, lambda d: pair_copy(ln, d, lax.rem(here + d, n), here).wait_send())
        )

    def pair_wait(ln):
        n, _, here = pair_place(ln)

        def one(d):
            frm = lax.rem(here - d + n, n)
            pair_copy(ln, d, frm, frm).wait_recv()

        looped(1, n, one)

    def hop(hops, step, s, whole=False):
        block = other if step == 2 else c
        to = other if step == 1 else peer
        ref = hops.buf.at[block] if whole else hops.buf.at[block, s]
        return remote(ref, ref, hops.sent.at[step, s], hops.came.at[step, s], i, to)

    def v_start(f):
        hop(f.v, 1, 0, True).start()
        hop(f.v, 0, 0, True).start()

    def v_forward(f):
        hop(f.v, 1, 0, True).wait_recv()
        hop(f.v, 2, 0, True).start()
        pending.append(lambda: [hop(f.v, step, 0, True).wait_send() for step in range(3)])

    def z_start(f, source):
        def one(s):
            piece = source[pl.ds(pl.multiple_of(s * SUB, SUB), SUB), :]
            f.z.buf[c, s] = piece.astype(F32).T.astype(BF16)
            hop(f.z, 0, s).start()

        def first(s):
            one(s)
            hop(f.z, 1, s).start()

        looped(0, SUBS - 1, first)
        one(SUBS - 1)

        def each(s):
            for step in range(3):
                hop(f.z, step, s).wait_send()

        pending.append(lambda: looped(0, SUBS, each))

    def z_apply(f, block, out, step):
        def one(s):
            if step is not None:
                hop(f.z, step, s).wait_recv()
                if step == 1:
                    hop(f.z, 2, s).start()
            out[...] += dot(f.z.buf[block, s], f.d[block, pl.ds(pl.multiple_of(s * SUB, SUB), SUB), :])

        if step is None:
            out[...] = jnp.zeros(out.shape, F32)
        looped(0, SUBS, one)

    def within(sm, n):
        return remote(sm.a.src.at[n], sm.a.dst.at[n], sm.a.sent.at[n], sm.a.came.at[n], i, peer)

    def between(sm, n):
        return remote(sm.b.src.at[n], sm.b.dst.at[n], sm.b.sent.at[n], sm.b.came.at[n], i, other)

    def a_pieces(sm, n, dest, piece):
        subs = sm.b.dst.shape[0]

        def one(p):
            out = piece(dest, p).astype(BF16)
            if subs == 1:
                sm.a.src[n] = out
            else:
                sm.a.src[n * subs + 2 * p] = out[:SUB]
                sm.a.src[n * subs + 2 * p + 1] = out[SUB:]

        looped(0, max(subs // 2, 1), one)

    def a_send(sm, n):
        subs = sm.b.dst.shape[0]
        looped(0, subs, lambda s: within(sm, n * subs + s).start())

    def own_pieces(sm, into, dest, piece):
        subs = sm.b.dst.shape[0]

        def one(p):
            out = piece(dest, p)
            if subs == 1:
                into[0] = out
            else:
                into[2 * p] = out[:SUB]
                into[2 * p + 1] = out[SUB:]

        looped(0, max(subs // 2, 1), one)

    def b_make(sm, held):
        def one(s):
            within(sm, s).wait_recv()
            sm.b.src[s] = (held[s] + sm.a.dst[s].astype(F32)).astype(BF16)

        looped(0, sm.b.dst.shape[0], one)

    def away(sm, piece, sent, ready=lambda n: None):
        ready(0)
        for p in range(SUBS // 2):
            out = piece(diag, p).astype(BF16)
            for k in range(2):
                sm.a.src[2 * p + k] = out[k * SUB : (k + 1) * SUB]
                within(sm, 2 * p + k).start()
        ready(1)
        for p in range(SUBS // 2):
            out = piece(other, p)
            for k in range(2):
                s = 2 * p + k
                within(sm, s).wait_recv()
                sm.b.src[s] = (out[k * SUB : (k + 1) * SUB] + sm.a.dst[s].astype(F32)).astype(BF16)
                if s < sent:
                    between(sm, s).start()

    def b_send(sm, lo, hi):
        looped(lo, hi, lambda s: between(sm, s).start())
        if hi == sm.b.dst.shape[0]:
            subs = hi

            def each(s):
                within(sm, s).wait_send()
                within(sm, subs + s).wait_send()
                between(sm, s).wait_send()

            pending.append(lambda: looped(0, subs, each))

    def b_acc(f):
        return m.bacc.at[0] if f is child else m.bacc.at[1]

    def b_sums(f):
        piece, acc = b_piece(f), b_acc(f)
        a_pieces(f.bsum, 0, diag, piece)
        a_send(f.bsum, 0)
        a_pieces(f.bsum, 1, peer, piece)
        a_send(f.bsum, 1)
        own_pieces(f.bsum, acc, other, piece)
        b_make(f.bsum, acc)
        b_send(f.bsum, 0, 1)
        own_pieces(f.bsum, acc, c, piece)

    def sum_wait(sm, s, acc):
        subs = sm.b.dst.shape[0]
        within(sm, subs + s).wait_recv()
        between(sm, s).wait_recv()
        return acc[s] + sm.a.dst[subs + s].astype(F32) + sm.b.dst[s].astype(F32)

    def d_piece(f, rhs):
        def piece(dest, s):
            return dot(f.d[dest, pl.ds(pl.multiple_of(s * 2 * SUB, 2 * SUB), 2 * SUB), :], rhs[...])

        return piece

    def b_piece(f):
        def piece(dest, s):
            out = dot(f.d[dest], f.ut[...])
            return jnp.concatenate([out[: NLOC // 2], out[NLOC // 2 :]], axis=1)

        return piece

    def b_finish(f):
        packed = sum_wait(f.bsum, 0, b_acc(f))
        out = jnp.concatenate([packed[:, :RANK], packed[:, RANK:]], axis=0)
        f.bl[...] = out.astype(BF16)
        high, low = high_low(out.T)
        f.fhl[:RANK] = high
        f.fhl[RANK:] = low

    def make_e(f):
        def add(block):
            f.e[...] += dot(f.v.buf[block], f.d[block])

        f.e[...] = dot(f.v.buf[c], f.d[c])
        v_forward(f)
        add(other)
        hop(f.v, 0, 0, True).wait_recv()
        add(peer)
        hop(f.v, 2, 0, True).wait_recv()
        add(diag)
        high, low = high_low(f.e[...])
        f.ehl[:RANK] = high
        f.ehl[RANK:] = low

    def project(pair, vec):
        both = dot(pair[...], vec)
        return both[:RANK] + both[RANK:]

    def pack(a):
        return jnp.concatenate([a[: RANK // 2], a[RANK // 2 :]], axis=1)

    def unpack(a):
        return jnp.concatenate([a[:, :HS], a[:, HS:]], axis=0)

    def scan_one(sc, partial):
        for k in range(COLS):
            sc.part.src[k] = pack(partial[:, k * HS : (k + 1) * HS]).astype(BF16)
        twin_send(sc.part)

    def scan_two(sc):
        here = pair_place(sc.rows)[2]
        for k, total in enumerate(twin_wait(sc.part)):
            sc.rows.dst[here, k] = total.astype(BF16)
        pair_send(sc.rows)

    def scan_three(sc):
        pair_wait(sc.rows)
        both = dot(sc.phl[...], sc.rows.dst[...].reshape(sc.phl.shape[1], 2 * HS))
        both = both[: 2 * RANK] + both[2 * RANK :]
        send_state(sc.state, both[:RANK, :HS] + both[RANK:, HS:])

    def send_state(ln, state):
        ln.dst[c] = pack(state).astype(BF16)
        col_send(ln)

    def wait_state(ln):
        col_wait(ln)
        return jnp.concatenate([unpack(ln.dst[k].astype(F32)) for k in range(COLS)], axis=1).astype(BF16)

    def split_phi(sc):
        high, low = high_low(sc.phi[...].T)
        sc.phl[: 2 * RANK] = high
        sc.phl[2 * RANK :] = low

    def kernel_send(f, kernel_part, source):
        for k in range(COLS):
            if source is None:
                f.kern.src[k] = pack(kernel_part).astype(BF16)
            else:
                f.kern.src[k] = jnp.concatenate([source[:, k * HS : (k + 1) * HS], kernel_part], axis=1).astype(BF16)
        twin_send(f.kern)

    def route_values(rt, values):
        rt.rows.src[...] = values.astype(BF16).reshape(rt.rows.src.shape)
        rt.rows.dst[i] = rt.rows.src[i]

    def route_rows(rt, values):
        route_values(rt, values)
        row_send(rt.rows)

    def route_cols(rt):
        rt.cols.dst[c] = rt.cols.src[c]
        col_send(rt.cols)

    def rows_of(rt):
        row_wait(rt.rows)
        return rt.rows.dst[...].reshape(ROWS * 32, rt.rows.dst.shape[2])

    def onehot(shape, axis, at):
        return (lax.broadcasted_iota(jnp.int32, shape, axis) == at).astype(BF16)

    def load(f, hbm, n):
        return pltpu.make_async_copy(hbm.at[dests[n]], f.d.at[dests[n]], f.loaded.at[n])

    load_rc = pltpu.make_async_copy(rc_hbm, m.rc, m.near.at[0])
    load_rp = pltpu.make_async_copy(rp_hbm, m.rp, m.near.at[1])
    load_w = pltpu.make_async_copy(
        w_hbm.at[pl.ds(pl.multiple_of(lax.div(c, 2) * 2 * GROUPS, 2 * GROUPS), 2 * GROUPS), :], m.w16, m.near.at[2]
    )
    load_rc.start()
    for n in range(COLS):
        load(child, dc_hbm, n).start()
    for n in range(COLS):
        load(parent, dp_hbm, n).start()
    load_w.start()
    load_rp.start()

    barrier = pltpu.get_barrier_semaphore()

    def greet(row, col):
        pl.semaphore_signal(barrier, inc=1, device_id=(row, col), device_id_type=MESH)

    looped(1, ROWS, lambda d: greet(lax.rem(i + d, ROWS), c))
    for d in range(1, COLS):
        greet(i, lax.rem(c + d, COLS))
        greet(twin, lax.rem(c + d, COLS))

    m.trans.dst[side] = jnp.concatenate([pc[...], pp[...]], axis=1)
    child.v.buf[c] = vc[...]
    parent.v.buf[c] = vp[...]
    pl.semaphore_wait(barrier, ROWS - 1 + 2 * (COLS - 1))

    v_start(child)
    v_start(parent)
    trans_copy = remote(
        m.trans.dst.at[side], m.trans.dst.at[side], m.trans.sent.at[0], m.trans.came.at[0], twin, c
    )
    trans_from = remote(
        m.trans.dst.at[1 - side], m.trans.dst.at[1 - side], m.trans.sent.at[0], m.trans.came.at[0], twin, c
    )
    trans_copy.start()
    pending.append(trans_copy.wait_send)
    load_rc.wait()
    for s in range(SUBS):
        m.rt[s * SUB : (s + 1) * SUB, :] = m.rc[:, s * SUB : (s + 1) * SUB].T.astype(BF16)
    child.ut[...] = uc[...].astype(F32).T.astype(BF16)
    y_part = d_piece(child, m.rt)
    away(child.ysum, y_part, 0, lambda n: load(child, dc_hbm, n).wait())
    eye = (
        lax.broadcasted_iota(jnp.int32, (RANK, RANK), 0) == lax.broadcasted_iota(jnp.int32, (RANK, RANK), 1)
    )
    eye_f = eye.astype(F32)
    left = lax.broadcasted_iota(jnp.int32, (RANK, 2 * RANK), 1) < RANK

    def iota(rows, cols, axis):
        return lax.broadcasted_iota(jnp.int32, (rows, cols), axis)

    def over_lanes(mask, values):
        return jnp.sum(jnp.where(mask, values, 0), axis=1, keepdims=True)

    def over_rows(mask, values):
        return jnp.sum(jnp.where(mask, values, 0), axis=0, keepdims=True)

    wide = iota(RANK, 512, 1)
    tall = iota(512, RANK, 0)

    listed = jnp.concatenate([entries[:, :RANK], entries[:, RANK:]], axis=0)
    held_here = ((listed >> 5) == i).astype(BF16)
    below = (iota(RANK, RANK, 0) < iota(RANK, RANK, 1)).astype(BF16)
    place = iota(ROWS, RANK, 0)
    code = dot(held_here, below).astype(jnp.int32) + 32 * (2 * (place & (HALF - 1)) + (place >> 4))
    wanted = i * 32 + (iota(RANK, RANK, 0) >> 1)
    second_half = iota(RANK, RANK, 0) & 1
    found = jnp.zeros((RANK, RANK), jnp.int32)
    for j in range(ROWS):
        hit = (listed[j : j + 1, :] == wanted) & (second_half == (2 * (j % HALF) + j // HALF) // HALF)
        found = found + jnp.where(hit, code[j : j + 1, :], 0)
    src_col = jnp.sum(found, axis=1, keepdims=True)
    src_row = over_rows(eye, src_col)
    src_tall = over_lanes(iota(512, RANK, 1) == (tall >> 3), src_row) + 4 * (iota(512, 1, 0) & 7)
    src_wide = over_rows(iota(RANK, 512, 0) == (wide >> 3), src_col) + 4 * (iota(1, 512, 1) & 7)
    m.sel_wide[...] = onehot((512, ROWS * 32), 1, src_tall)

    load(child, dc_hbm, 2).wait()
    load(child, dc_hbm, 3).wait()
    make_e(child)
    kernel_send(child, project(child.ehl, child.ut[...]), project(child.ehl, m.rt[...]))
    load_rp.wait()
    for k in range(COLS):
        m.swap.src[k] = m.rp[:, k * NLOC : (k + 1) * NLOC].astype(BF16)
    m.swap.dst[c] = m.swap.src[c]
    col_send(m.swap)
    b_send(child.ysum, 0, 1)
    a_pieces(child.ysum, 1, peer, y_part)
    a_send(child.ysum, 1)
    own_pieces(child.ysum, m.acc, c, y_part)
    parent.ut[...] = up[...].astype(F32).T.astype(BF16)
    trans_from.wait_recv()
    here = pair_place(child.maps)[2]
    for k, total in enumerate(twin_wait(child.kern)):
        transfer = m.trans.dst[k, :, :RANK] - total[:, RANK:]
        child.maps.dst[here, k] = jnp.concatenate([transfer, total[:, :RANK]], axis=1)
    pair_send(child.maps)
    for n in range(COLS):
        load(parent, dp_hbm, n).wait()
    make_e(parent)
    kernel_send(parent, project(parent.ehl, parent.ut[...]), None)
    b_send(child.ysum, 1, SUBS)
    b_sums(child)

    pairs = entries[pl.ds(lax.div(i, 2), 1), :] >> 5
    mine = jnp.where(side == 0, pairs[:, :RANK], pairs[:, RANK:])
    mine_col = over_lanes(eye, mine)
    earlier = (mine_col == mine) & (iota(RANK, RANK, 1) < iota(RANK, RANK, 0))
    tgt_col = mine_col * 32 + jnp.sum(earlier.astype(jnp.int32), axis=1, keepdims=True)
    tgt_row = over_rows(eye, tgt_col)
    tgt_tall = over_lanes(iota(512, RANK, 1) == (tall & (RANK - 1)), tgt_row) + 4 * (iota(512, 1, 0) >> 6)
    by_group = over_rows(iota(RANK, 512, 0) == (wide & (RANK - 1)), tgt_col) + 4 * (iota(1, 512, 1) >> 6)
    by_block = over_rows(iota(RANK, 512, 0) == (wide >> 3), tgt_col) + 4 * (iota(1, 512, 1) & 7)
    m.sel_tall[...] = onehot((ROWS * 32, 512), 0, by_block)
    load_w.wait()
    w16 = m.w16[...].astype(F32)
    w8 = jnp.where(lax.rem(c, 2) == 0, w16[:GROUPS], w16[GROUPS:])
    ws = jnp.concatenate([w8[:, b * BLK : (b + 1) * BLK] for b in range(RANK)], axis=0).astype(BF16)
    route_values(weights, dot(m.sel_tall[...], ws))
    m.sel_tall[...] = onehot((ROWS * 32, 512), 0, by_group)
    for g in range(GROUPS):
        cols = slice(g * BLK, (g + 1) * BLK)
        allowed = iota(RANK, BLK, 0) < ranks[g]
        m.msk[:, cols] = jnp.where(allowed, wf[:, cols].astype(F32), 0.0).astype(BF16)

    pair_wait(child.maps)

    def store_phi(sc, j, value):
        sc.phi[pl.ds(pl.multiple_of(j * (RANK // 2), RANK // 2), RANK // 2), :] = pack(value)

    def child_step(j, both):
        now = child.maps.dst[lax.div(j, 2), lax.rem(j, 2)]
        product = jnp.dot(now[:, :RANK], both, precision=HIGH)
        added = jnp.concatenate([now[:, RANK:], jnp.zeros((RANK, RANK), F32)], axis=1)
        store_phi(child_back, j, jnp.where(j > loc, both[:, RANK:], 0.0))
        moves = (left & (j < loc)) | (~left & (j > loc))
        return jnp.where(moves, product + added, both)

    both = lax.fori_loop(
        0, HALF, child_step, jnp.concatenate([jnp.zeros((RANK, RANK), F32), eye_f], axis=1), unroll=4
    )
    send_state(m.first, both[:, :RANK])
    here = pair_place(parent.maps)[2]
    for k, total in enumerate(twin_wait(parent.kern)):
        parent.maps.dst[here, k] = pack(m.trans.dst[k, :, RANK:]) - total
    pair_send(parent.maps)
    row_send(weights.rows)
    b_sums(parent)
    b_finish(child)
    h_child = wait_state(m.first)

    def child_y(s):
        rows = pl.ds(pl.multiple_of(s * SUB, SUB), SUB)
        value = sum_wait(child.ysum, s, m.acc) - dot(child.bl[rows, :], h_child)
        m.y[rows, :] = value
        m.yb[rows, :] = value.astype(BF16)

    looped(0, SUBS, child_y)
    for g in range(GROUPS):
        m.fac[g * RANK : (g + 1) * RANK, :] = dot(
            m.msk[:, g * BLK : (g + 1) * BLK], m.yb[g * BLK : (g + 1) * BLK, :]
        ).astype(BF16)
    route_rows(factors, dot(m.sel_tall[...], m.fac[...]))

    weights.cols.src[...] = dot(m.sel_wide[...], rows_of(weights)).astype(BF16).reshape(COLS, 128, BLK)
    route_cols(weights)
    pair_wait(parent.maps)

    def map_of(j):
        return unpack(parent.maps.dst[lax.div(j, 2), lax.rem(j, 2)])

    def falling_step(n, pair):
        out = []
        for start, now in ((ROWS, pair[0]), (HALF, pair[1])):
            j = start - 1 - n
            store_phi(ahead, j, jnp.where(j < i, now, 0.0).T)
            out.append(jnp.where(j < i, jnp.dot(now, map_of(j), precision=HIGH), now))
        return tuple(out)

    def rising_step(n, now):
        store_phi(back, n, jnp.where(n > i, now, 0.0))
        return jnp.where(n > i, jnp.dot(map_of(n), now, precision=HIGH), now)

    upper, _ = lax.fori_loop(0, HALF, falling_step, (eye_f, eye_f), unroll=4)
    for k in range(2):
        part = (slice(0, HALF * RANK // 2), slice(k * RANK, (k + 1) * RANK))
        ahead.phi[part] = lax.dot_general(
            ahead.phi[part], upper, (((1,), (1,)), ((), ())), precision=HIGH, preferred_element_type=F32
        )
    split_phi(ahead)
    col_wait(m.swap)
    for k in range(SUBS):
        cols = slice(k * SUB, (k + 1) * SUB)
        m.rpt[cols, :] = m.swap.dst[:, :, cols].astype(F32).reshape(H, SUB).T
    b_finish(parent)
    col_wait(weights.cols)

    factors.cols.src[...] = dot(m.sel_wide[...], rows_of(factors)).astype(BF16).reshape(COLS, 128, H)
    route_cols(factors)
    m.mskt[...] = m.msk[...].astype(F32).T.astype(BF16)
    m.sel_tall[...] = onehot((ROWS * 32, 512), 0, src_wide)
    m.sel_wide[...] = onehot((512, ROWS * 32), 1, tgt_tall)
    col_wait(factors.cols)

    def joined(ref, q):
        return jnp.concatenate([ref[k, q * 16 : (q + 1) * 16, :] for k in range(COLS)], axis=0)

    for q in range(GROUPS):
        rows = slice(q * BLK, (q + 1) * BLK)
        contrib = dot_tn(joined(weights.cols.dst, q), joined(factors.cols.dst, q))
        m.rpb[rows, :] = (m.rpt[rows, :] - contrib).astype(BF16)

    scan_one(ahead, project(parent.ehl, m.rpb[...]))
    y_part = d_piece(parent, m.rpb)
    away(parent.ysum, y_part, SUBS - 1)
    scan_two(ahead)
    a_pieces(parent.ysum, 1, peer, y_part)
    a_send(parent.ysum, 1)
    own_pieces(parent.ysum, m.acc, c, y_part)
    scan_three(ahead)
    b_send(parent.ysum, SUBS - 1, SUBS)
    lax.fori_loop(0, ROWS, rising_step, eye_f, unroll=4)
    split_phi(back)
    split_phi(child_back)
    h_parent = wait_state(ahead.state)

    def parent_y(s):
        rows = pl.ds(pl.multiple_of(s * SUB, SUB), SUB)
        m.rpb[rows, :] = (sum_wait(parent.ysum, s, m.acc) - dot(parent.bl[rows, :], h_parent)).astype(BF16)

    looped(0, SUBS, parent_y)
    scan_one(back, project(parent.fhl, m.rpb[...]))
    z_start(parent, m.rpb)
    z_apply(parent, c, m.xp, None)
    scan_two(back)
    z_apply(parent, peer, m.xp, 0)
    scan_three(back)
    hop(parent.z, 1, SUBS - 1).start()
    z_apply(parent, other, m.xp, 1)
    z_apply(parent, diag, m.xp, 2)
    g_parent = wait_state(back.state)
    m.xp[...] -= dot_tn(g_parent, parent.ehl[:RANK])
    store_xp = pltpu.make_async_copy(m.xp, xp_out, m.near.at[3])
    store_xp.start()
    pending.append(store_xp.wait)

    for q in range(GROUPS):
        values = dot_nt(joined(weights.cols.dst, q), m.xp[:, q * BLK : (q + 1) * BLK].astype(BF16)).astype(BF16)
        for k in range(COLS):
            pulled.cols.src[k, q * 16 : (q + 1) * 16, :] = values[k * 16 : (k + 1) * 16]
    route_cols(pulled)
    col_wait(pulled.cols)
    route_rows(pulled, dot(m.sel_tall[...], pulled.cols.dst[...].reshape(512, H)))
    m.fac[...] = dot(m.sel_wide[...], rows_of(pulled)).astype(BF16)
    for g in range(GROUPS):
        rows = slice(g * BLK, (g + 1) * BLK)
        correction = dot(m.mskt[rows, :], m.fac[g * RANK : (g + 1) * RANK, :])
        m.yb[rows, :] = (m.y[rows, :] - correction).astype(BF16)

    scan_one(child_back, project(child.fhl, m.yb[...]))
    z_start(child, m.yb)
    z_apply(child, c, m.rc, None)
    scan_two(child_back)
    z_apply(child, peer, m.rc, 0)
    scan_three(child_back)
    hop(child.z, 1, SUBS - 1).start()
    z_apply(child, other, m.rc, 1)
    z_apply(child, diag, m.rc, 2)
    g_child = wait_state(child_back.state)
    m.rc[...] -= dot_tn(g_child, child.ehl[:RANK])
    store_xc = pltpu.make_async_copy(m.rc, xc_out, m.near.at[4])
    store_xc.start()
    pending.append(store_xc.wait)
    for done in pending:
        done()


def hand_over(xc, xp, xc_out, xp_out, buf, arrive, leave):
    steps = []
    for k, (src, dst) in enumerate(((xc, xc_out), (xp, xp_out))):
        for q in range(SUBS):
            rows = pl.ds(q * HS, HS)
            steps.append(
                (
                    pltpu.make_async_copy(src.at[rows, :], buf.at[k, rows, :], arrive.at[k, q]),
                    pltpu.make_async_copy(buf.at[k, rows, :], dst.at[rows, :], leave.at[k, q]),
                )
            )
    for come, _ in steps:
        come.start()
    for come, go in steps:
        come.wait()
        go.start()
    for _, go in steps:
        go.wait()


def shards(
    rhs_child, rhs_parent, dinv_child, dinv_parent, ubase_child, vbase_child, ubase_parent, vbase_parent,
    trans_child, trans_parent, w_first, w_second, block_ranks, extend_map,
):
    vmem = pl.BlockSpec(memory_space=pltpu.VMEM)
    hbm = pl.BlockSpec(memory_space=pl.ANY)
    smem = pl.BlockSpec(memory_space=pltpu.SMEM)
    shapes = [jax.ShapeDtypeStruct((H, NLOC), F32)] * 2
    x_child, x_parent = pl.pallas_call(
        kernel,
        out_shape=shapes,
        in_specs=[hbm] * 5 + [vmem] * 8 + [smem],
        out_specs=[hbm, hbm],
        scratch_shapes=scratch_tree(),
        compiler_params=pltpu.CompilerParams(
            collective_id=0, has_side_effects=True, vmem_limit_bytes=60 * 1024 * 1024
        ),
    )(
        rhs_child,
        rhs_parent,
        dinv_child.reshape(COLS, NLOC, NLOC),
        dinv_parent.reshape(COLS, NLOC, NLOC),
        w_second,
        ubase_child,
        vbase_child,
        ubase_parent,
        vbase_parent,
        w_first,
        trans_child.reshape(RANK, RANK),
        trans_parent.reshape(RANK, RANK),
        extend_map.reshape(HALF, 2 * RANK),
        block_ranks,
    )
    return tuple(
        pl.pallas_call(
            hand_over,
            out_shape=shapes,
            in_specs=[hbm, hbm],
            out_specs=[hbm, hbm],
            scratch_shapes=[pltpu.VMEM((2, H, NLOC), F32), DMA((2, SUBS)), DMA((2, SUBS))],
        )(x_child, x_parent)
    )


def solution(mesh):
    return jax.shard_map(
        shards,
        mesh=mesh,
        in_specs=(
            P(None, ("row", "col")),
            P("col", "row"),
            P("row", "col"),
            P("row", "col"),
            P(None, ("row", "col")),
            P(None, ("row", "col")),
            P(None, ("row", "col")),
            P(None, ("row", "col")),
            P("row", None, None),
            P("row", None, None),
            P(None, ("row", "col")),
            P(None, "row"),
            P(("row", "col")),
            P(),
        ),
        out_specs=(P(None, ("row", "col")), P(None, ("row", "col"))),
        check_vma=False,
    )
```

```python
from typing import Any, NamedTuple

import jax
import jax.numpy as jnp
from jax import lax
from jax.experimental import pallas as pl
from jax.experimental.pallas import tpu as pltpu
from jax.sharding import PartitionSpec as P

MESH = pl.DeviceIdType.MESH
F32 = jnp.float32
BF16 = jnp.bfloat16
HIGH = lax.Precision.HIGHEST

ROWS = 32
COLS = 4
HALF = 16
H = 256
HS = 64
RANK = 64
NLOC = 1024
GROUPS = 8
BLK = 128
SUBS = 4
SUB = NLOC // SUBS
SLOTS = 4

DMA = pltpu.SemaphoreType.DMA


class Link(NamedTuple):
    src: Any
    dst: Any
    sent: Any
    came: Any


class Hops(NamedTuple):
    buf: Any
    sent: Any
    came: Any


class Sums(NamedTuple):
    a: Link
    b: Link


class Front(NamedTuple):
    d: Any
    loaded: Any
    ut: Any
    v: Hops
    e: Any
    ehl: Any
    fhl: Any
    bl: Any
    ysum: Sums
    bsum: Sums
    z: Hops
    kern: Link
    maps: Link


class Scan(NamedTuple):
    phi: Any
    phl: Any
    part: Link
    rows: Link
    state: Link


class Route(NamedTuple):
    rows: Link
    cols: Link


class Rest(NamedTuple):
    first: Link
    swap: Link
    sel_tall: Any
    sel_wide: Any
    acc: Any
    bacc: Any
    rt: Any
    rpt: Any
    rpb: Any
    y: Any
    yb: Any
    mskt: Any
    fac: Any
    msk: Any
    trans: Link
    rc: Any
    rp: Any
    w16: Any
    xp: Any
    near: Any


def link(src, dst, count, kind=BF16):
    source = None if src is None else pltpu.VMEM(src, kind)
    return Link(source, pltpu.VMEM(dst, kind), DMA((count,)), DMA((count,)))


def sums(subs, rows, lanes):
    two, one = (2 * subs, rows, lanes), (subs, rows, lanes)
    return Sums(link(two, two, 2 * subs), link(one, one, subs))


def front(count, tile):
    return Front(
        d=pltpu.VMEM((COLS, NLOC, NLOC), BF16),
        loaded=DMA((COLS,)),
        ut=pltpu.VMEM((NLOC, RANK), BF16),
        v=Hops(pltpu.VMEM((COLS, RANK, NLOC), BF16), DMA((3, 1)), DMA((3, 1))),
        e=pltpu.VMEM((RANK, NLOC), F32),
        ehl=pltpu.VMEM((2 * RANK, NLOC), BF16),
        fhl=pltpu.VMEM((2 * RANK, NLOC), BF16),
        bl=pltpu.VMEM((NLOC, RANK), BF16),
        ysum=sums(SUBS, SUB, H),
        bsum=sums(1, NLOC // 2, 2 * RANK),
        z=Hops(pltpu.VMEM((COLS, SUBS, H, SUB), BF16), DMA((3, SUBS)), DMA((3, SUBS))),
        kern=link((COLS,) + tile, (2 * COLS,) + tile, 2 * COLS),
        maps=link(None, (count // 2, 2) + tile, count // 2, F32),
    )


def scan(count):
    part = (RANK // 2, 2 * HS)
    return Scan(
        phi=pltpu.VMEM((count * RANK // 2, 2 * RANK), F32),
        phl=pltpu.VMEM((4 * RANK, count * RANK // 2), BF16),
        part=link((COLS,) + part, (2 * COLS,) + part, 2 * COLS),
        rows=link(None, (count // 2, 2) + part, count // 2),
        state=link(None, (COLS,) + part, COLS),
    )


def route(lanes):
    rows, cols = (ROWS, 32, lanes), (COLS, 128, lanes)
    return Route(link(rows, rows, ROWS), link(cols, cols, COLS))


def scratch_tree():
    part = (COLS, RANK // 2, 2 * HS)
    swap = (COLS, HS, NLOC)
    rest = Rest(
        first=link(None, part, COLS),
        swap=link(swap, swap, COLS),
        sel_tall=pltpu.VMEM((ROWS * 32, 512), BF16),
        sel_wide=pltpu.VMEM((512, ROWS * 32), BF16),
        acc=pltpu.VMEM((SUBS, SUB, H), F32),
        bacc=pltpu.VMEM((2, 1, NLOC // 2, 2 * RANK), F32),
        rt=pltpu.VMEM((NLOC, H), BF16),
        rpt=pltpu.VMEM((NLOC, H), F32),
        rpb=pltpu.VMEM((NLOC, H), BF16),
        y=pltpu.VMEM((NLOC, H), F32),
        yb=pltpu.VMEM((NLOC, H), BF16),
        mskt=pltpu.VMEM((NLOC, RANK), BF16),
        fac=pltpu.VMEM((512, H), BF16),
        msk=pltpu.VMEM((RANK, NLOC), BF16),
        trans=link(None, (2, RANK, 2 * RANK), 1, F32),
        rc=pltpu.VMEM((H, NLOC), F32),
        rp=pltpu.VMEM((HS, COLS * NLOC), F32),
        w16=pltpu.VMEM((2 * GROUPS, RANK * BLK), BF16),
        xp=pltpu.VMEM((H, NLOC), F32),
        near=DMA((8,)),
    )
    return (
        front(HALF, (RANK, 2 * RANK)), front(ROWS, (RANK // 2, 2 * RANK)), scan(ROWS), scan(ROWS), scan(HALF), route(H), route(BLK), route(H), rest,
    )


def dot(a, b):
    return jnp.dot(a, b, preferred_element_type=F32)


def dot_tn(a, b):
    return lax.dot_general(a, b, (((0,), (0,)), ((), ())), preferred_element_type=F32)


def dot_nt(a, b):
    return lax.dot_general(a, b, (((1,), (1,)), ((), ())), preferred_element_type=F32)


def high_low(a):
    high = a.astype(BF16)
    return high, (a - high.astype(F32)).astype(BF16)


def kernel(
    rc_hbm, rp_hbm, dc_hbm, dp_hbm, w_hbm, uc, vc, up, vp, wf, pc, pp, entries, ranks,
    xc_out, xp_out, child, parent, ahead, back, child_back, factors, weights, pulled, m,
):
    i = lax.axis_index("row")
    c = lax.axis_index("col")
    peer = c + 1 - 2 * lax.rem(c, 2)
    other = lax.rem(c + 2, COLS)
    diag = lax.rem(peer + 2, COLS)
    loc = lax.rem(i, HALF)
    base = i - loc
    side = lax.rem(i, 2)
    twin = i + 1 - 2 * side
    dests = (diag, other, peer, c)
    pending = []

    def remote(src, dst, ss, rs, row, col):
        return pltpu.make_async_remote_copy(
            src_ref=src, dst_ref=dst, send_sem=ss, recv_sem=rs, device_id=(row, col), device_id_type=MESH
        )

    def looped(lo, hi, fn):
        def one(s, carry):
            fn(s)
            return carry

        lax.fori_loop(lo, hi, one, 0)

    def piece_of(ln, here, to):
        return ln.dst.at[here] if ln.src is None else ln.src.at[to]

    def col_copy(ln, d, to, slot):
        return remote(piece_of(ln, c, to), ln.dst.at[slot], ln.sent.at[d], ln.came.at[d], i, to)

    def col_send(ln):
        for d in range(1, COLS):
            col_copy(ln, d, lax.rem(c + d, COLS), c).start()
        pending.append(lambda: [col_copy(ln, d, lax.rem(c + d, COLS), c).wait_send() for d in range(1, COLS)])

    def col_wait(ln):
        for d in range(1, COLS):
            frm = lax.rem(c - d + COLS, COLS)
            col_copy(ln, d, frm, frm).wait_recv()

    def row_place(ln):
        n = ln.dst.shape[0]
        return (n, base, loc) if n == HALF else (n, 0, i)

    def row_copy(ln, d, to, slot):
        _, start, here = row_place(ln)
        return remote(piece_of(ln, here, to), ln.dst.at[slot], ln.sent.at[d], ln.came.at[d], start + to, c)

    def row_send(ln):
        n, _, here = row_place(ln)
        looped(1, n, lambda d: row_copy(ln, d, lax.rem(here + d, n), here).start())
        pending.append(
            lambda: looped(1, n, lambda d: row_copy(ln, d, lax.rem(here + d, n), here).wait_send())
        )

    def row_wait(ln):
        n, _, here = row_place(ln)

        def one(d):
            frm = lax.rem(here - d + n, n)
            row_copy(ln, d, frm, frm).wait_recv()

        looped(1, n, one)

    def twin_copy(ln, n, to, slot, row):
        return remote(ln.src.at[to], ln.dst.at[slot], ln.sent.at[n], ln.came.at[n], row, to)

    def twin_send(ln):
        for d in range(1, COLS):
            twin_copy(ln, d, lax.rem(c + d, COLS), side * COLS + c, i).start()
        for d in range(COLS):
            twin_copy(ln, COLS + d, lax.rem(c + d, COLS), side * COLS + c, twin).start()

        def done():
            for d in range(1, COLS):
                twin_copy(ln, d, lax.rem(c + d, COLS), side * COLS + c, i).wait_send()
            for d in range(COLS):
                twin_copy(ln, COLS + d, lax.rem(c + d, COLS), side * COLS + c, twin).wait_send()

        pending.append(done)

    def twin_wait(ln):
        ln.dst[side * COLS + c] = ln.src[c]
        for d in range(1, COLS):
            frm = lax.rem(c - d + COLS, COLS)
            twin_copy(ln, d, frm, side * COLS + frm, i).wait_recv()
        for d in range(COLS):
            frm = lax.rem(c - d + COLS, COLS)
            twin_copy(ln, COLS + d, frm, (1 - side) * COLS + frm, twin).wait_recv()
        return [jnp.sum(ln.dst[k * COLS : (k + 1) * COLS].astype(F32), axis=0) for k in range(2)]

    def pair_place(ln):
        n = ln.dst.shape[0]
        return (n, base, lax.div(loc, 2)) if n == HALF // 2 else (n, 0, lax.div(i, 2))

    def pair_copy(ln, d, to, slot):
        _, start, here = pair_place(ln)
        return remote(
            ln.dst.at[here], ln.dst.at[slot], ln.sent.at[d], ln.came.at[d], start + 2 * to + side, c
        )

    def pair_send(ln):
        n, _, here = pair_place(ln)
        looped(1, n, lambda d: pair_copy(ln, d, lax.rem(here + d, n), here).start())
        pending.append(
            lambda: looped(1, n, lambda d: pair_copy(ln, d, lax.rem(here + d, n), here).wait_send())
        )

    def pair_wait(ln):
        n, _, here = pair_place(ln)

        def one(d):
            frm = lax.rem(here - d + n, n)
            pair_copy(ln, d, frm, frm).wait_recv()

        looped(1, n, one)

    def hop(hops, step, s, whole=False):
        block = other if step == 2 else c
        to = other if step == 1 else peer
        ref = hops.buf.at[block] if whole else hops.buf.at[block, s]
        return remote(ref, ref, hops.sent.at[step, s], hops.came.at[step, s], i, to)

    def v_start(f):
        hop(f.v, 1, 0, True).start()
        hop(f.v, 0, 0, True).start()

    def v_forward(f):
        hop(f.v, 1, 0, True).wait_recv()
        hop(f.v, 2, 0, True).start()
        pending.append(lambda: [hop(f.v, step, 0, True).wait_send() for step in range(3)])

    def z_start(f, source):
        def one(s):
            piece = source[pl.ds(pl.multiple_of(s * SUB, SUB), SUB), :]
            f.z.buf[c, s] = piece.astype(F32).T.astype(BF16)

        def first(s):
            one(s)
            hop(f.z, 1, s).start()
            hop(f.z, 0, s).start()

        looped(0, SUBS, first)

        def each(s):
            for step in range(3):
                hop(f.z, step, s).wait_send()

        pending.append(lambda: looped(0, SUBS, each))

    def z_apply(f, block, out, step):
        def one(s):
            if step is not None:
                hop(f.z, step, s).wait_recv()
                if step == 1:
                    hop(f.z, 2, s).start()
            out[...] += dot(f.z.buf[block, s], f.d[block, pl.ds(pl.multiple_of(s * SUB, SUB), SUB), :])

        if step is None:
            out[...] = jnp.zeros(out.shape, F32)
        looped(0, SUBS, one)

    def within(sm, n):
        return remote(sm.a.src.at[n], sm.a.dst.at[n], sm.a.sent.at[n], sm.a.came.at[n], i, peer)

    def between(sm, n):
        return remote(sm.b.src.at[n], sm.b.dst.at[n], sm.b.sent.at[n], sm.b.came.at[n], i, other)

    def a_pieces(sm, n, dest, piece):
        subs = sm.b.dst.shape[0]

        def one(p):
            out = piece(dest, p).astype(BF16)
            if subs == 1:
                sm.a.src[n] = out
            else:
                sm.a.src[n * subs + 2 * p] = out[:SUB]
                sm.a.src[n * subs + 2 * p + 1] = out[SUB:]

        looped(0, max(subs // 2, 1), one)

    def a_send(sm, n):
        subs = sm.b.dst.shape[0]
        looped(0, subs, lambda s: within(sm, n * subs + s).start())

    def own_pieces(sm, into, dest, piece):
        subs = sm.b.dst.shape[0]

        def one(p):
            out = piece(dest, p)
            if subs == 1:
                into[0] = out
            else:
                into[2 * p] = out[:SUB]
                into[2 * p + 1] = out[SUB:]

        looped(0, max(subs // 2, 1), one)

    def b_make(sm, held):
        def one(s):
            within(sm, s).wait_recv()
            sm.b.src[s] = (held[s] + sm.a.dst[s].astype(F32)).astype(BF16)

        looped(0, sm.b.dst.shape[0], one)

    def away(sm, piece, sent, ready=lambda n: None):
        ready(0)
        for p in range(SUBS // 2):
            out = piece(diag, p).astype(BF16)
            for k in range(2):
                sm.a.src[2 * p + k] = out[k * SUB : (k + 1) * SUB]
                within(sm, 2 * p + k).start()
        ready(1)
        for p in range(SUBS // 2):
            out = piece(other, p)
            for k in range(2):
                s = 2 * p + k
                within(sm, s).wait_recv()
                sm.b.src[s] = (out[k * SUB : (k + 1) * SUB] + sm.a.dst[s].astype(F32)).astype(BF16)
                if s < sent:
                    between(sm, s).start()

    def b_send(sm, lo, hi):
        looped(lo, hi, lambda s: between(sm, s).start())
        if hi == sm.b.dst.shape[0]:
            subs = hi

            def each(s):
                within(sm, s).wait_send()
                within(sm, subs + s).wait_send()
                between(sm, s).wait_send()

            pending.append(lambda: looped(0, subs, each))

    def b_acc(f):
        return m.bacc.at[0] if f is child else m.bacc.at[1]

    def b_sums(f):
        piece, acc = b_piece(f), b_acc(f)
        a_pieces(f.bsum, 0, diag, piece)
        a_send(f.bsum, 0)
        a_pieces(f.bsum, 1, peer, piece)
        a_send(f.bsum, 1)
        own_pieces(f.bsum, acc, other, piece)
        b_make(f.bsum, acc)
        b_send(f.bsum, 0, 1)
        own_pieces(f.bsum, acc, c, piece)

    def sum_wait(sm, s, acc):
        subs = sm.b.dst.shape[0]
        within(sm, subs + s).wait_recv()
        between(sm, s).wait_recv()
        return acc[s] + sm.a.dst[subs + s].astype(F32) + sm.b.dst[s].astype(F32)

    def d_piece(f, rhs):
        def piece(dest, s):
            return dot(f.d[dest, pl.ds(pl.multiple_of(s * 2 * SUB, 2 * SUB), 2 * SUB), :], rhs[...])

        return piece

    def b_piece(f):
        def piece(dest, s):
            out = dot(f.d[dest], f.ut[...])
            return jnp.concatenate([out[: NLOC // 2], out[NLOC // 2 :]], axis=1)

        return piece

    def b_finish(f):
        packed = sum_wait(f.bsum, 0, b_acc(f))
        out = jnp.concatenate([packed[:, :RANK], packed[:, RANK:]], axis=0)
        f.bl[...] = out.astype(BF16)
        high, low = high_low(out.T)
        f.fhl[:RANK] = high
        f.fhl[RANK:] = low

    def make_e(f):
        def add(block):
            f.e[...] += dot(f.v.buf[block], f.d[block])

        f.e[...] = dot(f.v.buf[c], f.d[c])
        v_forward(f)
        add(other)
        hop(f.v, 0, 0, True).wait_recv()
        add(peer)
        hop(f.v, 2, 0, True).wait_recv()
        add(diag)
        high, low = high_low(f.e[...])
        f.ehl[:RANK] = high
        f.ehl[RANK:] = low

    def project(pair, vec):
        both = dot(pair[...], vec)
        return both[:RANK] + both[RANK:]

    def pack(a):
        return jnp.concatenate([a[: RANK // 2], a[RANK // 2 :]], axis=1)

    def unpack(a):
        return jnp.concatenate([a[:, :HS], a[:, HS:]], axis=0)

    def scan_one(sc, partial):
        for k in range(COLS):
            sc.part.src[k] = pack(partial[:, k * HS : (k + 1) * HS]).astype(BF16)
        twin_send(sc.part)

    def scan_two(sc):
        here = pair_place(sc.rows)[2]
        for k, total in enumerate(twin_wait(sc.part)):
            sc.rows.dst[here, k] = total.astype(BF16)
        pair_send(sc.rows)

    def scan_three(sc):
        pair_wait(sc.rows)
        both = dot(sc.phl[...], sc.rows.dst[...].reshape(sc.phl.shape[1], 2 * HS))
        both = both[: 2 * RANK] + both[2 * RANK :]
        send_state(sc.state, both[:RANK, :HS] + both[RANK:, HS:])

    def send_state(ln, state):
        ln.dst[c] = pack(state).astype(BF16)
        col_send(ln)

    def wait_state(ln):
        col_wait(ln)
        return jnp.concatenate([unpack(ln.dst[k].astype(F32)) for k in range(COLS)], axis=1).astype(BF16)

    def split_phi(sc):
        high, low = high_low(sc.phi[...].T)
        sc.phl[: 2 * RANK] = high
        sc.phl[2 * RANK :] = low

    def kernel_send(f, kernel_part, source):
        for k in range(COLS):
            if source is None:
                f.kern.src[k] = pack(kernel_part).astype(BF16)
            else:
                f.kern.src[k] = jnp.concatenate([source[:, k * HS : (k + 1) * HS], kernel_part], axis=1).astype(BF16)
        twin_send(f.kern)

    def route_values(rt, values):
        rt.rows.src[...] = values.astype(BF16).reshape(rt.rows.src.shape)
        rt.rows.dst[i] = rt.rows.src[i]

    def route_rows(rt, values):
        route_values(rt, values)
        row_send(rt.rows)

    def route_cols(rt):
        rt.cols.dst[c] = rt.cols.src[c]
        col_send(rt.cols)

    def rows_of(rt):
        row_wait(rt.rows)
        return rt.rows.dst[...].reshape(ROWS * 32, rt.rows.dst.shape[2])

    def onehot(shape, axis, at):
        return (lax.broadcasted_iota(jnp.int32, shape, axis) == at).astype(BF16)

    def load(f, hbm, n):
        return pltpu.make_async_copy(hbm.at[dests[n]], f.d.at[dests[n]], f.loaded.at[n])

    load_rc = pltpu.make_async_copy(rc_hbm, m.rc, m.near.at[0])
    load_rp = pltpu.make_async_copy(rp_hbm, m.rp, m.near.at[1])
    load_w = pltpu.make_async_copy(
        w_hbm.at[pl.ds(pl.multiple_of(lax.div(c, 2) * 2 * GROUPS, 2 * GROUPS), 2 * GROUPS), :], m.w16, m.near.at[2]
    )
    load_rc.start()
    for n in range(COLS):
        load(child, dc_hbm, n).start()
    for n in range(COLS):
        load(parent, dp_hbm, n).start()
    load_w.start()
    load_rp.start()

    barrier = pltpu.get_barrier_semaphore()

    def greet(row, col):
        pl.semaphore_signal(barrier, inc=1, device_id=(row, col), device_id_type=MESH)

    looped(1, ROWS, lambda d: greet(lax.rem(i + d, ROWS), c))
    for d in range(1, COLS):
        greet(i, lax.rem(c + d, COLS))
        greet(twin, lax.rem(c + d, COLS))

    m.trans.dst[side] = jnp.concatenate([pc[...], pp[...]], axis=1)
    child.v.buf[c] = vc[...]
    parent.v.buf[c] = vp[...]
    pl.semaphore_wait(barrier, ROWS - 1 + 2 * (COLS - 1))

    v_start(child)
    v_start(parent)
    trans_copy = remote(
        m.trans.dst.at[side], m.trans.dst.at[side], m.trans.sent.at[0], m.trans.came.at[0], twin, c
    )
    trans_from = remote(
        m.trans.dst.at[1 - side], m.trans.dst.at[1 - side], m.trans.sent.at[0], m.trans.came.at[0], twin, c
    )
    trans_copy.start()
    pending.append(trans_copy.wait_send)
    load_rc.wait()
    for s in range(SUBS):
        m.rt[s * SUB : (s + 1) * SUB, :] = m.rc[:, s * SUB : (s + 1) * SUB].T.astype(BF16)
    child.ut[...] = uc[...].astype(F32).T.astype(BF16)
    y_part = d_piece(child, m.rt)
    away(child.ysum, y_part, 0, lambda n: load(child, dc_hbm, n).wait())
    eye = (
        lax.broadcasted_iota(jnp.int32, (RANK, RANK), 0) == lax.broadcasted_iota(jnp.int32, (RANK, RANK), 1)
    )
    eye_f = eye.astype(F32)
    left = lax.broadcasted_iota(jnp.int32, (RANK, 2 * RANK), 1) < RANK

    def iota(rows, cols, axis):
        return lax.broadcasted_iota(jnp.int32, (rows, cols), axis)

    def over_lanes(mask, values):
        return jnp.sum(jnp.where(mask, values, 0), axis=1, keepdims=True)

    def over_rows(mask, values):
        return jnp.sum(jnp.where(mask, values, 0), axis=0, keepdims=True)

    wide = iota(RANK, 512, 1)
    tall = iota(512, RANK, 0)

    listed = jnp.concatenate([entries[:, :RANK], entries[:, RANK:]], axis=0)
    held_here = ((listed >> 5) == i).astype(BF16)
    below = (iota(RANK, RANK, 0) < iota(RANK, RANK, 1)).astype(BF16)
    place = iota(ROWS, RANK, 0)
    code = dot(held_here, below).astype(jnp.int32) + 32 * (2 * (place & (HALF - 1)) + (place >> 4))
    wanted = i * 32 + (iota(RANK, RANK, 0) >> 1)
    second_half = iota(RANK, RANK, 0) & 1
    found = jnp.zeros((RANK, RANK), jnp.int32)
    for j in range(ROWS):
        hit = (listed[j : j + 1, :] == wanted) & (second_half == (2 * (j % HALF) + j // HALF) // HALF)
        found = found + jnp.where(hit, code[j : j + 1, :], 0)
    src_col = jnp.sum(found, axis=1, keepdims=True)
    src_row = over_rows(eye, src_col)
    src_tall = over_lanes(iota(512, RANK, 1) == (tall >> 3), src_row) + 4 * (iota(512, 1, 0) & 7)
    src_wide = over_rows(iota(RANK, 512, 0) == (wide >> 3), src_col) + 4 * (iota(1, 512, 1) & 7)
    m.sel_wide[...] = onehot((512, ROWS * 32), 1, src_tall)

    load(child, dc_hbm, 2).wait()
    load(child, dc_hbm, 3).wait()
    make_e(child)
    kernel_send(child, project(child.ehl, child.ut[...]), project(child.ehl, m.rt[...]))
    load_rp.wait()
    for k in range(COLS):
        m.swap.src[k] = m.rp[:, k * NLOC : (k + 1) * NLOC].astype(BF16)
    m.swap.dst[c] = m.swap.src[c]
    col_send(m.swap)
    b_send(child.ysum, 0, 1)
    a_pieces(child.ysum, 1, peer, y_part)
    a_send(child.ysum, 1)
    own_pieces(child.ysum, m.acc, c, y_part)
    parent.ut[...] = up[...].astype(F32).T.astype(BF16)
    trans_from.wait_recv()
    here = pair_place(child.maps)[2]
    for k, total in enumerate(twin_wait(child.kern)):
        transfer = m.trans.dst[k, :, :RANK] - total[:, RANK:]
        child.maps.dst[here, k] = jnp.concatenate([transfer, total[:, :RANK]], axis=1)
    pair_send(child.maps)
    for n in range(COLS):
        load(parent, dp_hbm, n).wait()
    make_e(parent)
    kernel_send(parent, project(parent.ehl, parent.ut[...]), None)
    b_send(child.ysum, 1, SUBS)
    b_sums(child)

    pairs = entries[pl.ds(lax.div(i, 2), 1), :] >> 5
    mine = jnp.where(side == 0, pairs[:, :RANK], pairs[:, RANK:])
    mine_col = over_lanes(eye, mine)
    earlier = (mine_col == mine) & (iota(RANK, RANK, 1) < iota(RANK, RANK, 0))
    tgt_col = mine_col * 32 + jnp.sum(earlier.astype(jnp.int32), axis=1, keepdims=True)
    tgt_row = over_rows(eye, tgt_col)
    tgt_tall = over_lanes(iota(512, RANK, 1) == (tall & (RANK - 1)), tgt_row) + 4 * (iota(512, 1, 0) >> 6)
    by_group = over_rows(iota(RANK, 512, 0) == (wide & (RANK - 1)), tgt_col) + 4 * (iota(1, 512, 1) >> 6)
    by_block = over_rows(iota(RANK, 512, 0) == (wide >> 3), tgt_col) + 4 * (iota(1, 512, 1) & 7)
    m.sel_tall[...] = onehot((ROWS * 32, 512), 0, by_block)
    load_w.wait()
    w16 = m.w16[...].astype(F32)
    w8 = jnp.where(lax.rem(c, 2) == 0, w16[:GROUPS], w16[GROUPS:])
    ws = jnp.concatenate([w8[:, b * BLK : (b + 1) * BLK] for b in range(RANK)], axis=0).astype(BF16)
    route_values(weights, dot(m.sel_tall[...], ws))
    m.sel_tall[...] = onehot((ROWS * 32, 512), 0, by_group)
    for g in range(GROUPS):
        cols = slice(g * BLK, (g + 1) * BLK)
        allowed = iota(RANK, BLK, 0) < ranks[g]
        m.msk[:, cols] = jnp.where(allowed, wf[:, cols].astype(F32), 0.0).astype(BF16)

    pair_wait(child.maps)

    def store_phi(sc, j, value):
        sc.phi[pl.ds(pl.multiple_of(j * (RANK // 2), RANK // 2), RANK // 2), :] = pack(value)

    def child_step(j, both):
        now = child.maps.dst[lax.div(j, 2), lax.rem(j, 2)]
        product = jnp.dot(now[:, :RANK], both, precision=HIGH)
        added = jnp.concatenate([now[:, RANK:], jnp.zeros((RANK, RANK), F32)], axis=1)
        store_phi(child_back, j, jnp.where(j > loc, both[:, RANK:], 0.0))
        moves = (left & (j < loc)) | (~left & (j > loc))
        return jnp.where(moves, product + added, both)

    both = lax.fori_loop(
        0, HALF, child_step, jnp.concatenate([jnp.zeros((RANK, RANK), F32), eye_f], axis=1), unroll=4
    )
    send_state(m.first, both[:, :RANK])
    here = pair_place(parent.maps)[2]
    for k, total in enumerate(twin_wait(parent.kern)):
        parent.maps.dst[here, k] = pack(m.trans.dst[k, :, RANK:]) - total
    pair_send(parent.maps)
    row_send(weights.rows)
    b_sums(parent)
    b_finish(child)
    h_child = wait_state(m.first)

    def child_y(s):
        rows = pl.ds(pl.multiple_of(s * SUB, SUB), SUB)
        value = sum_wait(child.ysum, s, m.acc) - dot(child.bl[rows, :], h_child)
        m.y[rows, :] = value
        m.yb[rows, :] = value.astype(BF16)

    looped(0, SUBS, child_y)
    for g in range(GROUPS):
        m.fac[g * RANK : (g + 1) * RANK, :] = dot(
            m.msk[:, g * BLK : (g + 1) * BLK], m.yb[g * BLK : (g + 1) * BLK, :]
        ).astype(BF16)
    route_rows(factors, dot(m.sel_tall[...], m.fac[...]))

    weights.cols.src[...] = dot(m.sel_wide[...], rows_of(weights)).astype(BF16).reshape(COLS, 128, BLK)
    route_cols(weights)
    pair_wait(parent.maps)

    def map_of(j):
        return unpack(parent.maps.dst[lax.div(j, 2), lax.rem(j, 2)])

    def falling_step(n, pair):
        out = []
        for start, now in ((ROWS, pair[0]), (HALF, pair[1])):
            j = start - 1 - n
            store_phi(ahead, j, jnp.where(j < i, now, 0.0).T)
            out.append(jnp.where(j < i, jnp.dot(now, map_of(j), precision=HIGH), now))
        return tuple(out)

    def rising_step(n, now):
        store_phi(back, n, jnp.where(n > i, now, 0.0))
        return jnp.where(n > i, jnp.dot(map_of(n), now, precision=HIGH), now)

    upper, _ = lax.fori_loop(0, HALF, falling_step, (eye_f, eye_f), unroll=4)
    for k in range(2):
        part = (slice(0, HALF * RANK // 2), slice(k * RANK, (k + 1) * RANK))
        ahead.phi[part] = lax.dot_general(
            ahead.phi[part], upper, (((1,), (1,)), ((), ())), precision=HIGH, preferred_element_type=F32
        )
    split_phi(ahead)
    col_wait(m.swap)
    for k in range(SUBS):
        cols = slice(k * SUB, (k + 1) * SUB)
        m.rpt[cols, :] = m.swap.dst[:, :, cols].astype(F32).reshape(H, SUB).T
    b_finish(parent)
    col_wait(weights.cols)

    factors.cols.src[...] = dot(m.sel_wide[...], rows_of(factors)).astype(BF16).reshape(COLS, 128, H)
    route_cols(factors)
    m.mskt[...] = m.msk[...].astype(F32).T.astype(BF16)
    m.sel_tall[...] = onehot((ROWS * 32, 512), 0, src_wide)
    m.sel_wide[...] = onehot((512, ROWS * 32), 1, tgt_tall)
    col_wait(factors.cols)

    def joined(ref, q):
        return jnp.concatenate([ref[k, q * 16 : (q + 1) * 16, :] for k in range(COLS)], axis=0)

    for q in range(GROUPS):
        rows = slice(q * BLK, (q + 1) * BLK)
        contrib = dot_tn(joined(weights.cols.dst, q), joined(factors.cols.dst, q))
        m.rpb[rows, :] = (m.rpt[rows, :] - contrib).astype(BF16)

    scan_one(ahead, project(parent.ehl, m.rpb[...]))
    y_part = d_piece(parent, m.rpb)
    away(parent.ysum, y_part, SUBS - 1)
    scan_two(ahead)
    a_pieces(parent.ysum, 1, peer, y_part)
    a_send(parent.ysum, 1)
    own_pieces(parent.ysum, m.acc, c, y_part)
    scan_three(ahead)
    b_send(parent.ysum, SUBS - 1, SUBS)
    lax.fori_loop(0, ROWS, rising_step, eye_f, unroll=4)
    split_phi(back)
    split_phi(child_back)
    h_parent = wait_state(ahead.state)

    def parent_y(s):
        rows = pl.ds(pl.multiple_of(s * SUB, SUB), SUB)
        m.rpb[rows, :] = (sum_wait(parent.ysum, s, m.acc) - dot(parent.bl[rows, :], h_parent)).astype(BF16)

    looped(0, SUBS, parent_y)
    scan_one(back, project(parent.fhl, m.rpb[...]))
    z_start(parent, m.rpb)
    z_apply(parent, c, m.xp, None)
    scan_two(back)
    z_apply(parent, peer, m.xp, 0)
    scan_three(back)
    z_apply(parent, other, m.xp, 1)
    z_apply(parent, diag, m.xp, 2)
    g_parent = wait_state(back.state)
    m.xp[...] -= dot_tn(g_parent, parent.ehl[:RANK])
    store_xp = pltpu.make_async_copy(m.xp, xp_out, m.near.at[3])
    store_xp.start()
    pending.append(store_xp.wait)

    for q in range(GROUPS):
        values = dot_nt(joined(weights.cols.dst, q), m.xp[:, q * BLK : (q + 1) * BLK].astype(BF16)).astype(BF16)
        for k in range(COLS):
            pulled.cols.src[k, q * 16 : (q + 1) * 16, :] = values[k * 16 : (k + 1) * 16]
    route_cols(pulled)
    col_wait(pulled.cols)
    route_rows(pulled, dot(m.sel_tall[...], pulled.cols.dst[...].reshape(512, H)))
    m.fac[...] = dot(m.sel_wide[...], rows_of(pulled)).astype(BF16)
    for g in range(GROUPS):
        rows = slice(g * BLK, (g + 1) * BLK)
        correction = dot(m.mskt[rows, :], m.fac[g * RANK : (g + 1) * RANK, :])
        m.yb[rows, :] = (m.y[rows, :] - correction).astype(BF16)

    scan_one(child_back, project(child.fhl, m.yb[...]))
    sent_before = list(pending)
    pending.clear()
    z_start(child, m.yb)
    z_apply(child, c, m.rc, None)
    scan_two(child_back)
    for done in sent_before:
        done()
    z_apply(child, peer, m.rc, 0)
    scan_three(child_back)
    z_apply(child, other, m.rc, 1)
    z_apply(child, diag, m.rc, 2)
    g_child = wait_state(child_back.state)
    m.rc[...] -= dot_tn(g_child, child.ehl[:RANK])
    store_xc = pltpu.make_async_copy(m.rc, xc_out, m.near.at[4])
    store_xc.start()
    pending.append(store_xc.wait)
    for done in pending:
        done()


def hand_over(xc, xp, xc_out, xp_out, buf, arrive, leave):
    steps = []
    for k, (src, dst) in enumerate(((xc, xc_out), (xp, xp_out))):
        for q in range(SUBS):
            rows = pl.ds(q * HS, HS)
            steps.append(
                (
                    pltpu.make_async_copy(src.at[rows, :], buf.at[k, rows, :], arrive.at[k, q]),
                    pltpu.make_async_copy(buf.at[k, rows, :], dst.at[rows, :], leave.at[k, q]),
                )
            )
    for come, _ in steps:
        come.start()
    for come, go in steps:
        come.wait()
        go.start()
    for _, go in steps:
        go.wait()


def shards(
    rhs_child, rhs_parent, dinv_child, dinv_parent, ubase_child, vbase_child, ubase_parent, vbase_parent,
    trans_child, trans_parent, w_first, w_second, block_ranks, extend_map,
):
    vmem = pl.BlockSpec(memory_space=pltpu.VMEM)
    hbm = pl.BlockSpec(memory_space=pl.ANY)
    smem = pl.BlockSpec(memory_space=pltpu.SMEM)
    shapes = [jax.ShapeDtypeStruct((H, NLOC), F32)] * 2
    x_child, x_parent = pl.pallas_call(
        kernel,
        out_shape=shapes,
        in_specs=[hbm] * 5 + [vmem] * 8 + [smem],
        out_specs=[hbm, hbm],
        scratch_shapes=scratch_tree(),
        compiler_params=pltpu.CompilerParams(
            collective_id=0, has_side_effects=True, vmem_limit_bytes=60 * 1024 * 1024
        ),
    )(
        rhs_child,
        rhs_parent,
        dinv_child.reshape(COLS, NLOC, NLOC),
        dinv_parent.reshape(COLS, NLOC, NLOC),
        w_second,
        ubase_child,
        vbase_child,
        ubase_parent,
        vbase_parent,
        w_first,
        trans_child.reshape(RANK, RANK),
        trans_parent.reshape(RANK, RANK),
        extend_map.reshape(HALF, 2 * RANK),
        block_ranks,
    )
    return tuple(
        pl.pallas_call(
            hand_over,
            out_shape=shapes,
            in_specs=[hbm, hbm],
            out_specs=[hbm, hbm],
            scratch_shapes=[pltpu.VMEM((2, H, NLOC), F32), DMA((2, SUBS)), DMA((2, SUBS))],
        )(x_child, x_parent)
    )


def solution(mesh):
    return jax.shard_map(
        shards,
        mesh=mesh,
        in_specs=(
            P(None, ("row", "col")),
            P("col", "row"),
            P("row", "col"),
            P("row", "col"),
            P(None, ("row", "col")),
            P(None, ("row", "col")),
            P(None, ("row", "col")),
            P(None, ("row", "col")),
            P("row", None, None),
            P("row", None, None),
            P(None, ("row", "col")),
            P(None, "row"),
            P(("row", "col")),
            P(),
        ),
        out_specs=(P(None, ("row", "col")), P(None, ("row", "col"))),
        check_vma=False,
    )
```
